512 devices in a mesh: wide: 32 (over x, z_hi, core), narrow: 16 (over z_lo, y).
Axes of the slice: x: 4, y: 4, z: 16 (z_hi: 4, z_lo: 4; z = z_hi * 4 + z_lo), core: 2. Of those that a mesh axis runs over, the one named last changes fastest.
Arguments:
- chaos_field: float32 [64, 4, 256, 455], P('wide', None, 'narrow'), may hold values from -2.4 to 2.4
- mean_conductivity: float32 [64, 4, 256], P('wide', None, 'narrow'), may hold values from 0.5 to 2
- kl_fields: float32 [12, 64, 4, 256], P(None, 'wide', None, 'narrow'), may hold values from -1.5 to 1.5
- pairs: int32 [12, 91, 3], replicated, may hold values from 0 to 454, as said below
Outputs:
- applied: float32 [64, 4, 256, 455], P('wide', None, 'narrow')
The draws below stay inside these ranges and needn't reach their ends.
Inputs may be any that keep to these rules, and one draw needn't show every extreme that they name: `pairs`: the first two entries of each row are mode numbers; each random variable's rows name each mode of total degree below 3 once as lower and the mode raised by one in that variable as raised; the third entry is that degree, 1 to 3. The modes are numbered in an order drawn from the seed.
All inputs are finite; a program needn't handle non-finite values.
Results may differ from the reference program's by a relative error of at most 0.0001.
Values sent between devices are 32-bit elements; how exact they have to be, the bound alone decides.
No kernel may reach another device: no remote copies, remote signals or barrier semaphores. Data moves between devices by JAX's collectives and lax.ppermute only.
A program may use at most 64 MiB of HBM per device.

```python
import math
import jax
import jax.numpy as jnp
import numpy as np
from jax import lax

KL = 12
DEGREE = 3
MODES = 455
NZ = 4
NY = 64
NX = 256


def enumerate_modes(count, degree):
    if count == 0:
        return [()]
    result = []
    for leading in range(degree + 1):
        for remainder in enumerate_modes(count - 1, degree - leading):
            result.append((leading,) + remainder)
    return result


def triple_table(count, degree):
    modes = sorted(enumerate_modes(count, degree), key=sum)
    position = {}
    for number, mode in enumerate(modes):
        position[mode] = number
    lowers = []
    uppers = []
    levels = []
    for variable in range(count):
        for mode in modes:
            if sum(mode) < degree:
                raised = list(mode)
                raised[variable] = raised[variable] + 1
                lowers.append(position[mode])
                uppers.append(position[tuple(raised)])
                levels.append(raised[variable])
    shape_out = (count, len(lowers) // count)
    return (np.array(lowers).reshape(shape_out), np.array(uppers).reshape(shape_out), np.array(levels).reshape(shape_out))


def draw_pairs(key, part):
    key = jax.random.fold_in(key, 7)
    lowers, uppers, levels = triple_table(KL, DEGREE)
    relabel = jax.random.permutation(key, MODES).astype(jnp.int32)
    return jnp.stack([relabel[lowers], relabel[uppers], jnp.asarray(levels, jnp.int32)], axis=-1)


def block_scale(own_key, dims, pieces, low, top_value):
    def one(axis_at, parts):
        steps = jax.random.uniform(jax.random.fold_in(jax.random.fold_in(own_key, 6), axis_at), (parts,), jnp.float32, low / len(pieces), top_value / len(pieces))
        return jnp.repeat(jnp.exp(steps), dims[axis_at] // parts).reshape((-1,) + (1,) * (len(dims) - axis_at - 1))

    loudness = one(*pieces[0])
    for cut in pieces[1:]:
        loudness = loudness * one(*cut)
    return loudness


def scatter_about(own_key, shape, scale, most, pieces=(), held_as=jnp.bfloat16):
    values = scale * jax.random.normal(own_key, shape, jnp.float32)
    if pieces:
        values = values * block_scale(own_key, shape, pieces, -0.22, 0.18)
    return jnp.clip(values, -most, most).astype(held_as)


def setup_inputs(seed: int = 0) -> dict:
    seeds = jax.random.split(jax.random.key(seed), 5)
    return {
        "chaos_field": scatter_about(seeds[0], (NY, NZ, NX, MODES), 0.3, 2.4, ((0, 32), (2, 16)), jnp.float32),
        "mean_conductivity": jnp.clip(jnp.exp(math.log(2.0) - 1.3862944 * jax.random.uniform(seeds[1], (NY, NZ, NX), jnp.float32) ** block_scale(seeds[1], (NY, NZ, NX), ((0, 32), (2, 16)), -0.2, 0.2)), 0.5, 2.0),
        "kl_fields": scatter_about(seeds[2], (KL, NY, NZ, NX), 0.25, 1.5, ((1, 32), (3, 16)), jnp.float32),
        "pairs": draw_pairs(jax.random.fold_in(seeds[4], 71), 0),
    }


def contract(difference, center, kl_face, lower_index, upper_index, scaling):
    kl_last = jnp.moveaxis(kl_face, 0, -1)
    variables = kl_last.shape[-1]
    columns = lower_index.shape[0]
    owner = jnp.arange(columns) // (columns // variables)
    onehot = (jnp.arange(variables)[:, None] == owner[None, :]).astype(jnp.float32)
    weights = jnp.einsum('...k,kq->...q', kl_last, onehot, precision=lax.Precision.HIGHEST) * scaling
    upper_part = jnp.take(difference, upper_index, axis=-1) * weights
    lower_part = jnp.take(difference, lower_index, axis=-1) * weights
    flux = center[..., None] * difference
    flux = flux.at[..., lower_index].add(upper_part)
    return flux.at[..., upper_index].add(lower_part)

def forward(values, direction):
    size = values.shape[direction]
    kept = lax.slice_in_dim(values, 1, size, axis=direction)
    zeros = jnp.zeros_like(lax.slice_in_dim(values, 0, 1, axis=direction))
    return jnp.concatenate([kept, zeros], axis=direction)

def backward(values, direction):
    size = values.shape[direction]
    kept = lax.slice_in_dim(values, 0, size - 1, axis=direction)
    zeros = jnp.zeros_like(lax.slice_in_dim(values, 0, 1, axis=direction))
    return jnp.concatenate([zeros, kept], axis=direction)

def reference(chaos_field, mean_conductivity, kl_fields, pairs):
    lower_index = pairs[:, :, 0].reshape(-1).astype(jnp.int32)
    upper_index = pairs[:, :, 1].reshape(-1).astype(jnp.int32)
    scaling = jnp.sqrt(pairs[:, :, 2].reshape(-1).astype(jnp.float32))
    coefficients = jnp.concatenate([mean_conductivity[None], kl_fields], axis=0)
    applied = jnp.zeros_like(chaos_field)
    for direction in range(3):
        difference = chaos_field - forward(chaos_field, direction)
        face_coef = 0.5 * (coefficients + forward(coefficients, direction + 1))

        def one_row(packed):
            return contract(packed[0], packed[1], packed[2], lower_index, upper_index, scaling)
        flux = lax.map(one_row, (difference, face_coef[0], jnp.moveaxis(face_coef[1:], 1, 0)))
        applied = applied + flux - backward(flux, direction)
    return applied
```

```python
import functools

import jax
import jax.numpy as jnp
from jax import lax
from jax.experimental import pallas as pl
from jax.experimental.pallas import tpu as pltpu
from jax.sharding import PartitionSpec as P

F32, BF16 = jnp.float32, jnp.bfloat16
LANES = 128
ROWS, DEPTH, COLS = 2, 4, 16
ROW_CELLS = DEPTH * COLS
CELLS = ROWS * ROW_CELLS
GROUPS = ROWS * DEPTH
WIDTH = 512
COEF = 72


def split(x):
    hi = x.astype(BF16)
    lo = (x - hi.astype(F32)).astype(BF16)
    return jnp.concatenate([hi, lo], axis=0)


def dot(a, b):
    return jnp.dot(a, b, preferred_element_type=F32)


def dot_t(a, b):
    return lax.dot_general(a, b, (((1,), (1,)), ((), ())), preferred_element_type=F32)


def pack_kernel(modes, f_ref, mean_ref, kl_ref, wide1_ref, wide2_ref, nar1_ref, nar2_ref, all_ref):
    variables = kl_ref.shape[0]
    w_odd = lax.rem(lax.axis_index("wide"), 2)
    n_odd = lax.rem(lax.axis_index("narrow"), 2)
    slabs = []
    for g in range(GROUPS):
        r, z = divmod(g, DEPTH)
        slabs.append(mean_ref[r, z : z + 1, :])
        slabs.append(kl_ref[:, r, z, :])
        slabs.append(jnp.zeros((COLS - 1 - variables, COLS), F32))
    stacked = jnp.concatenate(slabs, axis=0)
    stacked = jnp.concatenate([stacked, jnp.zeros((CELLS, LANES - COLS), F32)], axis=1)
    turned = stacked.T[:COLS]
    lane = lax.broadcasted_iota(jnp.int32, (COLS, LANES), 1)
    inside = (lane >= COEF) & (lane < COEF + variables + 1)
    last = WIDTH - LANES
    for g in range(GROUPS):
        r, z = divmod(g, DEPTH)
        part = pltpu.roll(turned, (COEF - g * COLS) % LANES, axis=1)
        all_ref[g * COLS : (g + 1) * COLS, last:] = jnp.where(inside, part, 0.0)
    for r in range(ROWS):
        all_ref[r * ROW_CELLS : (r + 1) * ROW_CELLS, :modes] = f_ref[r]
    wide1_ref[...] = all_ref[pl.ds(pl.multiple_of(w_odd * ROW_CELLS, ROW_CELLS), ROW_CELLS), :]
    wide2_ref[...] = all_ref[pl.ds(pl.multiple_of((1 - w_odd) * ROW_CELLS, ROW_CELLS), ROW_CELLS), :]
    for g in range(GROUPS):
        ref = wide1_ref if g < DEPTH else wide2_ref
        at = g % DEPTH * COLS
        first = ref[at : at + 1, :]
        final = ref[at + COLS - 1 : at + COLS, :]
        nar1_ref[g : g + 1, :] = jnp.where(n_odd == 1, final, first)
        nar2_ref[g : g + 1, :] = jnp.where(n_odd == 1, first, final)


def pack(field, mean, kl):
    shape = jax.ShapeDtypeStruct
    vmem = pl.BlockSpec(memory_space=pltpu.VMEM)
    return pl.pallas_call(
        functools.partial(pack_kernel, field.shape[-1]),
        out_shape=(
            shape((ROW_CELLS, WIDTH), F32),
            shape((ROW_CELLS, WIDTH), F32),
            shape((GROUPS, WIDTH), F32),
            shape((GROUPS, WIDTH), F32),
        ),
        in_specs=[vmem] * 3,
        out_specs=[vmem] * 4,
        scratch_shapes=[pltpu.VMEM((CELLS, WIDTH), F32)],
        name="pack",
    )(field, mean, kl)


def modes_of(ref, modes):
    x = ref[...]
    lane = lax.broadcasted_iota(jnp.int32, x.shape, 1)
    return jnp.where(lane < modes, x, 0.0)


def coefs_of(ref):
    return ref[:, WIDTH - LANES :]


def column(coefs, k):
    return jnp.broadcast_to(coefs[:, COEF + k : COEF + k + 1], coefs.shape)


def tables(pairs_ref, pick_ref, place_ref, level_ref):
    variables, _, count = pairs_ref.shape
    mode = lax.broadcasted_iota(jnp.int32, (WIDTH, LANES), 0)
    lane = lax.broadcasted_iota(jnp.int32, (1, LANES), 1)
    used = lane < count

    def row(k, c):
        values = jnp.concatenate(
            [pairs_ref[k, c : c + 1, :], jnp.zeros((1, LANES - count), jnp.int32)], axis=1
        )
        return values

    low = jnp.where(used, row(0, 0), -1)
    low_column = jnp.broadcast_to(low, (LANES, LANES)).T
    eye = jnp.where(used & (low_column == low), 1.0, 0.0).astype(BF16)
    hot = jnp.where(mode == low, 1.0, 0.0).astype(BF16)
    pick_ref[:, :LANES] = hot
    place_ref[:LANES, :] = dot_t(eye, hot).astype(BF16)
    for k in range(variables):
        same = jnp.where(used & (low_column == row(k, 0)), 1.0, 0.0).astype(BF16)
        raised = jnp.where(mode == jnp.where(used, row(k, 1), -1), 1.0, 0.0).astype(BF16)
        levels = jnp.broadcast_to(jnp.where(used, row(k, 2), 0).astype(F32), (16, LANES)).astype(BF16)
        at = (k + 1) * LANES
        pick_ref[:, at : at + LANES] = dot_t(raised, same).astype(BF16)
        place_ref[at : at + LANES, :] = dot_t(same, raised).astype(BF16)
        level_ref[k * 8 : (k + 1) * 8, :] = jnp.sqrt(dot_t(levels, same)[:8])


def inner_kernel(modes, a_ref, b_ref, nar1_ref, nar2_ref, pairs_ref, pick_ref, place_ref, level_ref, side_ref,
                 low_ref, center_ref, picked_ref):
    variables = pairs_ref.shape[0]
    n_index = lax.axis_index("narrow")
    n_odd = lax.rem(n_index, 2)
    tables(pairs_ref, pick_ref, place_ref, level_ref)

    u = jnp.concatenate([modes_of(a_ref, modes), modes_of(b_ref, modes)], axis=0)
    c = jnp.concatenate([coefs_of(a_ref), coefs_of(b_ref)], axis=0)
    n1, n2 = nar1_ref[...], nar2_ref[...]
    before = jnp.where(n_odd == 1, n2, n1)
    behind = jnp.where(n_odd == 1, n1, n2)
    lane8 = lax.broadcasted_iota(jnp.int32, before.shape, 1)
    edge = jnp.concatenate([before, behind], axis=0)
    edge_u = jnp.concatenate(
        [jnp.where(lane8 < modes, before, 0.0), jnp.where(lane8 < modes, behind, 0.0)], axis=0
    )
    edge_c = edge[:, WIDTH - LANES :]
    rows = CELLS + 2 * GROUPS
    both = dot(split(jnp.concatenate([u, edge_u], axis=0)), pick_ref[...])
    picked_ref[...] = both[:rows] + both[rows:]

    face_y = 0.5 * (c[:ROW_CELLS] + c[ROW_CELLS:])
    zero = jnp.zeros((COLS, LANES), F32)

    def up_z(x):
        return jnp.concatenate(
            [x[COLS:ROW_CELLS], zero, x[ROW_CELLS + COLS :], zero], axis=0
        )

    def down_z(x):
        return jnp.concatenate(
            [zero, x[: ROW_CELLS - COLS], zero, x[ROW_CELLS : CELLS - COLS]], axis=0
        )

    face_z = 0.5 * (c + up_z(c))
    cell = lax.broadcasted_iota(jnp.int32, (CELLS, LANES), 0)
    not_last = lax.rem(cell, COLS) < COLS - 1
    face_x = jnp.where(not_last, 0.5 * (c + pltpu.roll(c, CELLS - 1, axis=0)), 0.0)

    def strip(get):
        return jnp.concatenate(
            [get(slice(g * COLS, g * COLS + 1)) for g in range(GROUPS)]
            + [get(slice((g + 1) * COLS - 1, (g + 1) * COLS)) for g in range(GROUPS)],
            axis=0,
        )

    edge_face = 0.5 * (strip(lambda s: c[s]) + edge_c)
    row16 = lax.broadcasted_iota(jnp.int32, edge_face.shape, 0)
    edge_face = jnp.where((n_index == 0) & (row16 < GROUPS), 0.0, edge_face)

    def weighted(k, dy, dz, dx):
        fy = column(face_y, k) * dy
        fz = column(face_z, k) * dz
        fx = column(face_x, k) * dx
        net = fz - down_z(fz) + fx - pltpu.roll(fx, 1, axis=0)
        return net + jnp.concatenate([fy, -fy], axis=0)

    def diffs(x):
        return (
            x[:ROW_CELLS] - x[ROW_CELLS:],
            x - up_z(x),
            x - pltpu.roll(x, CELLS - 1, axis=0),
        )

    def edge_diff(x, e):
        return strip(lambda s: x[s]) - e

    def add_edge(ref, lanes, value):
        for g in range(GROUPS):
            ref[g * COLS : g * COLS + 1, lanes] += value[g : g + 1]
            s = (g + 1) * COLS - 1
            ref[s : s + 1, lanes] += value[GROUPS + g : GROUPS + g + 1]

    for t in range(WIDTH // LANES):
        lanes = slice(t * LANES, (t + 1) * LANES)
        x = u[:, lanes]
        center_ref[:, lanes] = weighted(0, *diffs(x))
        add_edge(center_ref, lanes, column(edge_face, 0) * edge_diff(x, edge_u[:, lanes]))

    low = picked_ref[:CELLS, :LANES]
    low_diffs = diffs(low)
    low_edge = edge_diff(low, picked_ref[CELLS:, :LANES])
    low_sum = jnp.zeros((CELLS, LANES), F32)
    low_edge_sum = jnp.zeros((2 * GROUPS, LANES), F32)
    for k in range(1, variables + 1):
        lanes = slice(k * LANES, (k + 1) * LANES)
        out = slice((k - 1) * LANES, k * LANES)
        level = level_ref[(k - 1) * 8 : (k - 1) * 8 + 1, :]
        side_ref[:, out] = weighted(k, *low_diffs)
        add_edge(side_ref, out, column(edge_face, k) * low_edge)
        x = picked_ref[:CELLS, lanes]
        low_sum = low_sum + level * weighted(k, *diffs(x))
        low_edge_sum = low_edge_sum + level * (
            column(edge_face, k) * edge_diff(x, picked_ref[CELLS:, lanes])
        )
    low_ref[...] = low_sum
    add_edge(low_ref, slice(0, LANES), low_edge_sum)


def inner(modes, a, b, n1, n2, turned_pairs):
    shape = jax.ShapeDtypeStruct
    vmem = pl.BlockSpec(memory_space=pltpu.VMEM)
    variables = turned_pairs.shape[0]
    blocks = (variables + 1) * LANES
    return pl.pallas_call(
        functools.partial(inner_kernel, modes),
        out_shape=(
            shape((WIDTH, blocks), BF16),
            shape((blocks, WIDTH), BF16),
            shape((8 * variables, LANES), F32),
            shape((CELLS, variables * LANES), F32),
            shape((CELLS, LANES), F32),
            shape((CELLS, WIDTH), F32),
        ),
        in_specs=[vmem] * 5,
        out_specs=[vmem] * 6,
        scratch_shapes=[pltpu.VMEM((CELLS + 2 * GROUPS, blocks), F32)],
        compiler_params=pltpu.CompilerParams(vmem_limit_bytes=40 * 1024 * 1024),
        cost_estimate=pl.CostEstimate(flops=2_000_000_000, bytes_accessed=10_000_000, transcendentals=0),
        name="inner",
    )(a, b, n1, n2, turned_pairs)


def outer_kernel(modes, a_ref, b_ref, ha_ref, hb_ref, pick_ref, place_ref, level_ref, side_ref, low_ref,
                 center_ref, out_ref, terms_ref):
    variables = side_ref.shape[1] // LANES
    w_index = lax.axis_index("wide")
    w_odd = lax.rem(w_index, 2)
    d = jnp.concatenate(
        [modes_of(a_ref, modes) - modes_of(ha_ref, modes), modes_of(b_ref, modes) - modes_of(hb_ref, modes)], axis=0
    )
    face_a = 0.5 * (coefs_of(a_ref) + coefs_of(ha_ref))
    face_a = jnp.where(w_index == 0, 0.0, face_a)
    face = jnp.concatenate([face_a, 0.5 * (coefs_of(b_ref) + coefs_of(hb_ref))], axis=0)
    both = dot(split(d), pick_ref[...])
    picked = both[:CELLS] + both[CELLS:]
    low = picked[:, :LANES]
    low_sum = low_ref[...]
    for k in range(1, variables + 1):
        level = level_ref[(k - 1) * 8 : (k - 1) * 8 + 1, :]
        f = column(face, k)
        low_sum = low_sum + level * (f * picked[:, k * LANES : (k + 1) * LANES])
        side = level * (side_ref[:, (k - 1) * LANES : k * LANES] + f * low)
        terms_ref[:, k * LANES : (k + 1) * LANES] = split(side)
    terms_ref[:, :LANES] = split(low_sum)
    spread = dot(terms_ref[...], place_ref[...])
    f = column(face, 0)
    f = jnp.concatenate([f] * (WIDTH // LANES), axis=1)
    total = center_ref[...] + f * d + spread[:CELLS] + spread[CELLS:]
    out_ref[pl.ds(w_odd, 1)] = total[None, :ROW_CELLS, :modes]
    out_ref[pl.ds(1 - w_odd, 1)] = total[None, ROW_CELLS:, :modes]


def outer(modes, a, b, ha, hb, parts):
    vmem = pl.BlockSpec(memory_space=pltpu.VMEM)
    blocks = parts[0].shape[1]
    return pl.pallas_call(
        functools.partial(outer_kernel, modes),
        out_shape=jax.ShapeDtypeStruct((ROWS, ROW_CELLS, modes), F32),
        in_specs=[vmem] * 10,
        out_specs=vmem,
        scratch_shapes=[pltpu.VMEM((2 * CELLS, blocks), BF16)],
        compiler_params=pltpu.CompilerParams(vmem_limit_bytes=40 * 1024 * 1024),
        name="outer",
    )(a, b, ha, hb, *parts)


def exchange(block, axis, first):
    route = []
    for i in range(first, lax.axis_size(axis) - 1, 2):
        route += [(i, i + 1), (i + 1, i)]
    return lax.ppermute(block, axis, route)


def per_device(chaos_field, mean_conductivity, kl_fields, pairs):
    modes = chaos_field.shape[-1]
    field = chaos_field.reshape(ROWS, ROW_CELLS, modes)
    a, b, n1, n2 = pack(field, mean_conductivity, kl_fields)
    halo_a = exchange(a, "wide", 1)
    edge_1 = exchange(n1, "narrow", 1)
    edge_2 = exchange(n2, "narrow", 0)
    halo_b = exchange(b, "wide", 0)
    parts = inner(modes, a, b, edge_1, edge_2, pairs.transpose(0, 2, 1))
    out = outer(modes, a, b, halo_a, halo_b, parts)
    return out.reshape(chaos_field.shape)


def solution(mesh):
    placed = (
        P("wide", None, "narrow", None),
        P("wide", None, "narrow"),
        P(None, "wide", None, "narrow"),
        P(),
    )
    return jax.shard_map(
        per_device,
        mesh=mesh,
        in_specs=placed,
        out_specs=P("wide", None, "narrow", None),
        check_vma=False,
    )
```

```python
import functools

import jax
import jax.numpy as jnp
from jax import lax
from jax.experimental import pallas as pl
from jax.experimental.pallas import tpu as pltpu
from jax.sharding import PartitionSpec as P

F32, BF16 = jnp.float32, jnp.bfloat16
LANES = 128
ROWS, DEPTH, COLS = 2, 4, 16
ROW_CELLS = DEPTH * COLS
CELLS = ROWS * ROW_CELLS
GROUPS = ROWS * DEPTH
WIDTH = 512
HBM = pl.BlockSpec(memory_space=pltpu.HBM)
COEF = 72


def split(x):
    hi = x.astype(BF16)
    lo = (x - hi.astype(F32)).astype(BF16)
    return jnp.concatenate([hi, lo], axis=0)


def dot(a, b):
    return jnp.dot(a, b, preferred_element_type=F32)


def dot_t(a, b):
    return lax.dot_general(a, b, (((1,), (1,)), ((), ())), preferred_element_type=F32)


def fetch(sources, targets, sems):
    copies = [pltpu.make_async_copy(s, t, sems.at[i]) for i, (s, t) in enumerate(zip(sources, targets))]
    for copy in copies:
        copy.start()
    for copy in copies:
        copy.wait()


def pack_kernel(modes, f_hbm, mean_hbm, kl_hbm, wide1_ref, wide2_ref, nar1_ref, nar2_ref, all_ref, f_ref, mean_ref,
                kl_ref, sems):
    fetch((f_hbm, mean_hbm, kl_hbm), (f_ref, mean_ref, kl_ref), sems)
    variables = kl_ref.shape[0]
    w_odd = lax.rem(lax.axis_index("wide"), 2)
    n_odd = lax.rem(lax.axis_index("narrow"), 2)
    slabs = []
    for g in range(GROUPS):
        r, z = divmod(g, DEPTH)
        slabs.append(mean_ref[r, z : z + 1, :])
        slabs.append(kl_ref[:, r, z, :])
        slabs.append(jnp.zeros((COLS - 1 - variables, COLS), F32))
    stacked = jnp.concatenate(slabs, axis=0)
    stacked = jnp.concatenate([stacked, jnp.zeros((CELLS, LANES - COLS), F32)], axis=1)
    turned = stacked.T[:COLS]
    lane = lax.broadcasted_iota(jnp.int32, (COLS, LANES), 1)
    inside = (lane >= COEF) & (lane < COEF + variables + 1)
    last = WIDTH - LANES
    for g in range(GROUPS):
        r, z = divmod(g, DEPTH)
        part = pltpu.roll(turned, (COEF - g * COLS) % LANES, axis=1)
        all_ref[g * COLS : (g + 1) * COLS, last:] = jnp.where(inside, part, 0.0)
    for r in range(ROWS):
        all_ref[r * ROW_CELLS : (r + 1) * ROW_CELLS, :modes] = f_ref[r]
    wide1_ref[...] = all_ref[pl.ds(pl.multiple_of(w_odd * ROW_CELLS, ROW_CELLS), ROW_CELLS), :]
    wide2_ref[...] = all_ref[pl.ds(pl.multiple_of((1 - w_odd) * ROW_CELLS, ROW_CELLS), ROW_CELLS), :]
    for g in range(GROUPS):
        ref = wide1_ref if g < DEPTH else wide2_ref
        at = g % DEPTH * COLS
        first = ref[at : at + 1, :]
        final = ref[at + COLS - 1 : at + COLS, :]
        nar1_ref[g : g + 1, :] = jnp.where(n_odd == 1, final, first)
        nar2_ref[g : g + 1, :] = jnp.where(n_odd == 1, first, final)


def pack(field, mean, kl):
    shape = jax.ShapeDtypeStruct
    vmem = pl.BlockSpec(memory_space=pltpu.VMEM)
    return pl.pallas_call(
        functools.partial(pack_kernel, field.shape[-1]),
        out_shape=(
            shape((ROW_CELLS, WIDTH), F32),
            shape((ROW_CELLS, WIDTH), F32),
            shape((GROUPS, WIDTH), F32),
            shape((GROUPS, WIDTH), F32),
        ),
        in_specs=[HBM] * 3,
        out_specs=[vmem] * 4,
        scratch_shapes=[pltpu.VMEM((CELLS, WIDTH), F32)]
        + [pltpu.VMEM(x.shape, F32) for x in (field, mean, kl)]
        + [pltpu.SemaphoreType.DMA((3,))],
        compiler_params=pltpu.CompilerParams(vmem_limit_bytes=60 * 1024 * 1024),
        name="pack",
    )(field, mean, kl)


def modes_of(ref, modes):
    x = ref[...]
    lane = lax.broadcasted_iota(jnp.int32, x.shape, 1)
    return jnp.where(lane < modes, x, 0.0)


def coefs_of(ref):
    return ref[:, WIDTH - LANES :]


def column(coefs, k):
    return jnp.broadcast_to(coefs[:, COEF + k : COEF + k + 1], coefs.shape)


def tables_kernel(pairs_hbm, pick_ref, place_ref, level_ref, pairs_ref, sems):
    fetch((pairs_hbm,), (pairs_ref,), sems)
    variables, _, count = pairs_ref.shape
    mode = lax.broadcasted_iota(jnp.int32, (WIDTH, LANES), 0)
    lane = lax.broadcasted_iota(jnp.int32, (1, LANES), 1)
    used = lane < count

    def row(k, c):
        values = jnp.concatenate(
            [pairs_ref[k, c : c + 1, :], jnp.zeros((1, LANES - count), jnp.int32)], axis=1
        )
        return values

    low = jnp.where(used, row(0, 0), -1)
    low_column = jnp.broadcast_to(low, (LANES, LANES)).T
    eye = jnp.where(used & (low_column == low), 1.0, 0.0).astype(BF16)
    hot = jnp.where(mode == low, 1.0, 0.0).astype(BF16)
    pick_ref[:, :LANES] = hot
    place_ref[:LANES, :] = dot_t(eye, hot).astype(BF16)
    for k in range(variables):
        same = jnp.where(used & (low_column == row(k, 0)), 1.0, 0.0).astype(BF16)
        raised = jnp.where(mode == jnp.where(used, row(k, 1), -1), 1.0, 0.0).astype(BF16)
        levels = jnp.broadcast_to(jnp.where(used, row(k, 2), 0).astype(F32), (16, LANES)).astype(BF16)
        at = (k + 1) * LANES
        pick_ref[:, at : at + LANES] = dot_t(raised, same).astype(BF16)
        place_ref[at : at + LANES, :] = dot_t(same, raised).astype(BF16)
        level_ref[k * 8 : (k + 1) * 8, :] = jnp.sqrt(dot_t(levels, same)[:8])


def tables(turned_pairs):
    shape = jax.ShapeDtypeStruct
    vmem = pl.BlockSpec(memory_space=pltpu.VMEM)
    variables = turned_pairs.shape[0]
    blocks = (variables + 1) * LANES
    return pl.pallas_call(
        tables_kernel,
        out_shape=(
            shape((WIDTH, blocks), BF16),
            shape((blocks, WIDTH), BF16),
            shape((8 * variables, LANES), F32),
        ),
        in_specs=[HBM],
        out_specs=[vmem] * 3,
        scratch_shapes=[pltpu.VMEM(turned_pairs.shape, jnp.int32), pltpu.SemaphoreType.DMA((1,))],
        cost_estimate=pl.CostEstimate(flops=1_000_000_000, bytes_accessed=4_000_000, transcendentals=0),
        compiler_params=pltpu.CompilerParams(vmem_limit_bytes=40 * 1024 * 1024),
        name="tables",
    )(turned_pairs)


def inner_kernel(modes, a_hbm, b_hbm, nar1_hbm, nar2_hbm, pick_ref, level_ref, side_ref, low_ref, center_ref,
                 picked_ref, a_ref, b_ref, nar1_ref, nar2_ref, sems):
    variables = side_ref.shape[1] // LANES
    n_index = lax.axis_index("narrow")
    n_odd = lax.rem(n_index, 2)
    n_end = lax.axis_size("narrow") - 1
    fetch(
        (a_hbm, b_hbm, other(nar1_hbm, "narrow", 1), other(nar2_hbm, "narrow", 0)),
        (a_ref, b_ref, nar1_ref, nar2_ref),
        sems,
    )

    u = jnp.concatenate([modes_of(a_ref, modes), modes_of(b_ref, modes)], axis=0)
    c = jnp.concatenate([coefs_of(a_ref), coefs_of(b_ref)], axis=0)
    n1, n2 = nar1_ref[...], nar2_ref[...]
    before = jnp.where(n_odd == 1, n2, n1)
    behind = jnp.where(n_index == n_end, 0.0, jnp.where(n_odd == 1, n1, n2))
    lane8 = lax.broadcasted_iota(jnp.int32, before.shape, 1)
    edge = jnp.concatenate([before, behind], axis=0)
    edge_u = jnp.concatenate(
        [jnp.where(lane8 < modes, before, 0.0), jnp.where(lane8 < modes, behind, 0.0)], axis=0
    )
    edge_c = edge[:, WIDTH - LANES :]
    rows = CELLS + 2 * GROUPS
    both = dot(split(jnp.concatenate([u, edge_u], axis=0)), pick_ref[...])
    picked_ref[...] = both[:rows] + both[rows:]

    face_y = 0.5 * (c[:ROW_CELLS] + c[ROW_CELLS:])
    zero = jnp.zeros((COLS, LANES), F32)

    def up_z(x):
        return jnp.concatenate(
            [x[COLS:ROW_CELLS], zero, x[ROW_CELLS + COLS :], zero], axis=0
        )

    def down_z(x):
        return jnp.concatenate(
            [zero, x[: ROW_CELLS - COLS], zero, x[ROW_CELLS : CELLS - COLS]], axis=0
        )

    face_z = 0.5 * (c + up_z(c))
    cell = lax.broadcasted_iota(jnp.int32, (CELLS, LANES), 0)
    not_last = lax.rem(cell, COLS) < COLS - 1
    face_x = jnp.where(not_last, 0.5 * (c + pltpu.roll(c, CELLS - 1, axis=0)), 0.0)

    def strip(get):
        return jnp.concatenate(
            [get(slice(g * COLS, g * COLS + 1)) for g in range(GROUPS)]
            + [get(slice((g + 1) * COLS - 1, (g + 1) * COLS)) for g in range(GROUPS)],
            axis=0,
        )

    edge_face = 0.5 * (strip(lambda s: c[s]) + edge_c)
    row16 = lax.broadcasted_iota(jnp.int32, edge_face.shape, 0)
    edge_face = jnp.where((n_index == 0) & (row16 < GROUPS), 0.0, edge_face)

    def weighted(k, dy, dz, dx):
        fy = column(face_y, k) * dy
        fz = column(face_z, k) * dz
        fx = column(face_x, k) * dx
        net = fz - down_z(fz) + fx - pltpu.roll(fx, 1, axis=0)
        return net + jnp.concatenate([fy, -fy], axis=0)

    def diffs(x):
        return (
            x[:ROW_CELLS] - x[ROW_CELLS:],
            x - up_z(x),
            x - pltpu.roll(x, CELLS - 1, axis=0),
        )

    def edge_diff(x, e):
        return strip(lambda s: x[s]) - e

    def add_edge(ref, lanes, value):
        for g in range(GROUPS):
            ref[g * COLS : g * COLS + 1, lanes] += value[g : g + 1]
            s = (g + 1) * COLS - 1
            ref[s : s + 1, lanes] += value[GROUPS + g : GROUPS + g + 1]

    for t in range(WIDTH // LANES):
        lanes = slice(t * LANES, (t + 1) * LANES)
        x = u[:, lanes]
        center_ref[:, lanes] = weighted(0, *diffs(x))
        add_edge(center_ref, lanes, column(edge_face, 0) * edge_diff(x, edge_u[:, lanes]))

    low = picked_ref[:CELLS, :LANES]
    low_diffs = diffs(low)
    low_edge = edge_diff(low, picked_ref[CELLS:, :LANES])
    low_sum = jnp.zeros((CELLS, LANES), F32)
    low_edge_sum = jnp.zeros((2 * GROUPS, LANES), F32)
    for k in range(1, variables + 1):
        lanes = slice(k * LANES, (k + 1) * LANES)
        out = slice((k - 1) * LANES, k * LANES)
        level = level_ref[(k - 1) * 8 : (k - 1) * 8 + 1, :]
        side_ref[:, out] = weighted(k, *low_diffs)
        add_edge(side_ref, out, column(edge_face, k) * low_edge)
        x = picked_ref[:CELLS, lanes]
        low_sum = low_sum + level * weighted(k, *diffs(x))
        low_edge_sum = low_edge_sum + level * (
            column(edge_face, k) * edge_diff(x, picked_ref[CELLS:, lanes])
        )
    low_ref[...] = low_sum
    add_edge(low_ref, slice(0, LANES), low_edge_sum)


def inner(modes, a, b, n1, n2, pick, level):
    shape = jax.ShapeDtypeStruct
    vmem = pl.BlockSpec(memory_space=pltpu.VMEM)
    blocks = pick.shape[1]
    return pl.pallas_call(
        functools.partial(inner_kernel, modes),
        out_shape=(
            shape((CELLS, blocks - LANES), F32),
            shape((CELLS, LANES), F32),
            shape((CELLS, WIDTH), F32),
        ),
        in_specs=[HBM] * 4 + [vmem] * 2,
        out_specs=[vmem] * 3,
        scratch_shapes=[
            pltpu.VMEM((CELLS + 2 * GROUPS, blocks), F32),
            pltpu.VMEM((ROW_CELLS, WIDTH), F32),
            pltpu.VMEM((ROW_CELLS, WIDTH), F32),
            pltpu.VMEM((GROUPS, WIDTH), F32),
            pltpu.VMEM((GROUPS, WIDTH), F32),
            pltpu.SemaphoreType.DMA((4,)),
        ],
        compiler_params=pltpu.CompilerParams(vmem_limit_bytes=40 * 1024 * 1024),
        cost_estimate=pl.CostEstimate(flops=2_000_000_000, bytes_accessed=10_000_000, transcendentals=0),
        name="inner",
    )(a, b, n1, n2, pick, level)


def outer_kernel(modes, a_hbm, b_hbm, ha_hbm, hb_hbm, pick_ref, place_ref, level_ref, side_ref, low_ref,
                 center_ref, out_ref, terms_ref, a_ref, b_ref, ha_ref, hb_ref, sems):
    variables = side_ref.shape[1] // LANES
    w_index = lax.axis_index("wide")
    w_odd = lax.rem(w_index, 2)
    fetch(
        (a_hbm, b_hbm, other(ha_hbm, "wide", 1), other(hb_hbm, "wide", 0)),
        (a_ref, b_ref, ha_ref, hb_ref),
        sems,
    )

    @pl.when(w_index == lax.axis_size("wide") - 1)
    def _():
        ha_ref[...] = jnp.zeros_like(ha_ref)

    d = jnp.concatenate(
        [modes_of(a_ref, modes) - modes_of(ha_ref, modes), modes_of(b_ref, modes) - modes_of(hb_ref, modes)], axis=0
    )
    face_a = 0.5 * (coefs_of(a_ref) + coefs_of(ha_ref))
    face_a = jnp.where(w_index == 0, 0.0, face_a)
    face = jnp.concatenate([face_a, 0.5 * (coefs_of(b_ref) + coefs_of(hb_ref))], axis=0)
    both = dot(split(d), pick_ref[...])
    picked = both[:CELLS] + both[CELLS:]
    low = picked[:, :LANES]
    low_sum = low_ref[...]
    for k in range(1, variables + 1):
        level = level_ref[(k - 1) * 8 : (k - 1) * 8 + 1, :]
        f = column(face, k)
        low_sum = low_sum + level * (f * picked[:, k * LANES : (k + 1) * LANES])
        side = level * (side_ref[:, (k - 1) * LANES : k * LANES] + f * low)
        terms_ref[:, k * LANES : (k + 1) * LANES] = split(side)
    terms_ref[:, :LANES] = split(low_sum)
    spread = dot(terms_ref[...], place_ref[...])
    f = column(face, 0)
    f = jnp.concatenate([f] * (WIDTH // LANES), axis=1)
    total = center_ref[...] + f * d + spread[:CELLS] + spread[CELLS:]
    out_ref[pl.ds(w_odd, 1)] = total[None, :ROW_CELLS, :modes]
    out_ref[pl.ds(1 - w_odd, 1)] = total[None, ROW_CELLS:, :modes]


def outer(modes, a, b, ha, hb, parts):
    vmem = pl.BlockSpec(memory_space=pltpu.VMEM)
    blocks = parts[0].shape[1]
    return pl.pallas_call(
        functools.partial(outer_kernel, modes),
        out_shape=jax.ShapeDtypeStruct((ROWS, ROW_CELLS, modes), F32),
        in_specs=[HBM] * 4 + [vmem] * 6,
        out_specs=vmem,
        scratch_shapes=[
            pltpu.VMEM((2 * CELLS, blocks), BF16),
            pltpu.VMEM((ROW_CELLS, WIDTH), F32),
            pltpu.VMEM((ROW_CELLS, WIDTH), F32),
            pltpu.VMEM((ROW_CELLS, WIDTH), F32),
            pltpu.VMEM((ROW_CELLS, WIDTH), F32),
            pltpu.SemaphoreType.DMA((4,)),
        ],
        compiler_params=pltpu.CompilerParams(vmem_limit_bytes=40 * 1024 * 1024),
        name="outer",
    )(a, b, ha, hb, *parts)


def pair_up(block, axis, first):
    size = lax.axis_size(axis)
    pairs = [[i, (i + 1) % size] for i in range(first, size, 2)]
    return lax.all_gather(block, axis, axis_index_groups=pairs)


def other(ref, axis, first):
    if ref.shape[0] == 1:
        return ref.at[0]
    return ref.at[lax.rem(lax.axis_index(axis) + first + 1, 2)]


def per_device(chaos_field, mean_conductivity, kl_fields, pairs):
    modes = chaos_field.shape[-1]
    field = chaos_field.reshape(ROWS, ROW_CELLS, modes)
    a, b, n1, n2 = pack(field, mean_conductivity, kl_fields)
    halo_a = pair_up(a, "wide", 1)
    edge_1 = pair_up(n1, "narrow", 1)
    edge_2 = pair_up(n2, "narrow", 0)
    halo_b = pair_up(b, "wide", 0)
    pick, place, level = tables(pairs.transpose(0, 2, 1))
    parts = inner(modes, a, b, edge_1, edge_2, pick, level)
    out = outer(modes, a, b, halo_a, halo_b, (pick, place, level) + tuple(parts))
    return out.reshape(chaos_field.shape)


def solution(mesh):
    placed = (
        P("wide", None, "narrow", None),
        P("wide", None, "narrow"),
        P(None, "wide", None, "narrow"),
        P(),
    )
    return jax.shard_map(
        per_device,
        mesh=mesh,
        in_specs=placed,
        out_specs=P("wide", None, "narrow", None),
        check_vma=False,
    )
```

```python
import functools

import jax
import jax.numpy as jnp
from jax import lax
from jax.experimental import pallas as pl
from jax.experimental.pallas import tpu as pltpu
from jax.sharding import PartitionSpec as P

F32, BF16 = jnp.float32, jnp.bfloat16
LANES = 128
ROWS, DEPTH, COLS = 2, 4, 16
ROW_CELLS = DEPTH * COLS
CELLS = ROWS * ROW_CELLS
GROUPS = ROWS * DEPTH
WIDTH = 512
HBM = pl.BlockSpec(memory_space=pltpu.HBM)
IN_VMEM = pl.BlockSpec(memory_space=pltpu.VMEM)
COEF = 72


def split(x):
    hi = x.astype(BF16)
    lo = (x - hi.astype(F32)).astype(BF16)
    return jnp.concatenate([hi, lo], axis=0)


def dot(a, b):
    return jnp.dot(a, b, preferred_element_type=F32)


def dot_t(a, b):
    return lax.dot_general(a, b, (((1,), (1,)), ((), ())), preferred_element_type=F32)


def fetch(sources, targets, sems):
    copies = [pltpu.make_async_copy(s, t, sems.at[i]) for i, (s, t) in enumerate(zip(sources, targets))]
    for copy in copies:
        copy.start()
    for copy in copies:
        copy.wait()


def pack_rows(modes, f_ref, mean_ref, kl_ref, low_ref, high_ref, first_ref, last_ref):
    variables = kl_ref.shape[0]
    slabs = []
    for g in range(GROUPS):
        r, z = divmod(g, DEPTH)
        slabs.append(mean_ref[r, z : z + 1, :])
        slabs.append(kl_ref[:, r, z, :])
        slabs.append(jnp.zeros((COLS - 1 - variables, COLS), F32))
    stacked = jnp.concatenate(slabs, axis=0)
    stacked = jnp.concatenate([stacked, jnp.zeros((CELLS, LANES - COLS), F32)], axis=1)
    turned = stacked.T[:COLS]
    lane = lax.broadcasted_iota(jnp.int32, (COLS, LANES), 1)
    inside = (lane >= COEF) & (lane < COEF + variables + 1)
    behind = WIDTH - LANES
    for g in range(GROUPS):
        r, z = divmod(g, DEPTH)
        part = pltpu.roll(turned, (COEF - g * COLS) % LANES, axis=1)
        row = (low_ref, high_ref)[r]
        row[z * COLS : (z + 1) * COLS, behind:] = jnp.where(inside, part, 0.0)
    low_ref[:, :modes] = f_ref[0]
    high_ref[:, :modes] = f_ref[1]
    for g in range(GROUPS):
        r, z = divmod(g, DEPTH)
        row, at = (low_ref, high_ref)[r], z * COLS
        first_ref[g : g + 1, :] = row[at : at + 1, :]
        last_ref[g : g + 1, :] = row[at + COLS - 1 : at + COLS, :]


def modes_of(ref, modes):
    x = ref[...]
    lane = lax.broadcasted_iota(jnp.int32, x.shape, 1)
    return jnp.where(lane < modes, x, 0.0)


def coefs_of(ref):
    return ref[:, WIDTH - LANES :]


def column(coefs, k):
    return jnp.broadcast_to(coefs[:, COEF + k : COEF + k + 1], coefs.shape)


def tables(pairs_ref, pick_ref, place_ref, level_ref):
    variables, _, count = pairs_ref.shape
    mode = lax.broadcasted_iota(jnp.int32, (WIDTH, LANES), 0)
    lane = lax.broadcasted_iota(jnp.int32, (1, LANES), 1)
    used = lane < count

    def row(k, c):
        values = jnp.concatenate(
            [pairs_ref[k, c : c + 1, :], jnp.zeros((1, LANES - count), jnp.int32)], axis=1
        )
        return values

    low = jnp.where(used, row(0, 0), -1)
    low_column = jnp.broadcast_to(low, (LANES, LANES)).T
    eye = jnp.where(used & (low_column == low), 1.0, 0.0).astype(BF16)
    hot = jnp.where(mode == low, 1.0, 0.0).astype(BF16)
    pick_ref[:, :LANES] = hot
    place_ref[:LANES, :] = dot_t(eye, hot).astype(BF16)
    for k in range(variables):
        same = jnp.where(used & (low_column == row(k, 0)), 1.0, 0.0).astype(BF16)
        raised = jnp.where(mode == jnp.where(used, row(k, 1), -1), 1.0, 0.0).astype(BF16)
        levels = jnp.broadcast_to(jnp.where(used, row(k, 2), 0).astype(F32), (16, LANES)).astype(BF16)
        at = (k + 1) * LANES
        pick_ref[:, at : at + LANES] = dot_t(raised, same).astype(BF16)
        place_ref[at : at + LANES, :] = dot_t(same, raised).astype(BF16)
        level_ref[k * 8 : (k + 1) * 8, :] = jnp.sqrt(dot_t(levels, same)[:8])


def start_kernel(modes, f_hbm, mean_hbm, kl_hbm, pairs_hbm, low_ref, high_ref, first_ref, last_ref, *refs):
    given, (f_ref, mean_ref, kl_ref, pairs_ref, picked_ref, sems) = refs[:6], refs[6:]
    fetch((f_hbm, mean_hbm, kl_hbm), (f_ref, mean_ref, kl_ref), sems)
    pack_rows(modes, f_ref, mean_ref, kl_ref, low_ref, high_ref, first_ref, last_ref)

    @pl.when(early())
    def _():
        fetch((pairs_hbm,), (pairs_ref,), sems)
        inner(modes, low_ref, high_ref, pairs_ref, *given, picked_ref)


def later_kernel(modes, low_ref, high_ref, pairs_hbm, *refs):
    given, (pairs_ref, picked_ref, sems) = refs[:6], refs[6:]

    @pl.when(jnp.logical_not(early()))
    def _():
        fetch((pairs_hbm,), (pairs_ref,), sems)
        inner(modes, low_ref, high_ref, pairs_ref, *given, picked_ref)


def inner(modes, a_ref, b_ref, pairs_ref, pick_ref, place_ref, level_ref, side_ref, low_ref, center_ref, picked_ref):
    variables = pairs_ref.shape[0]
    tables(pairs_ref, pick_ref, place_ref, level_ref)

    u = jnp.concatenate([modes_of(a_ref, modes), modes_of(b_ref, modes)], axis=0)
    c = jnp.concatenate([coefs_of(a_ref), coefs_of(b_ref)], axis=0)
    both = dot(split(u), pick_ref[...])
    picked_ref[...] = both[:CELLS] + both[CELLS:]

    face_y = 0.5 * (c[:ROW_CELLS] + c[ROW_CELLS:])
    zero = jnp.zeros((COLS, LANES), F32)

    def up_z(x):
        return jnp.concatenate(
            [x[COLS:ROW_CELLS], zero, x[ROW_CELLS + COLS :], zero], axis=0
        )

    def down_z(x):
        return jnp.concatenate(
            [zero, x[: ROW_CELLS - COLS], zero, x[ROW_CELLS : CELLS - COLS]], axis=0
        )

    face_z = 0.5 * (c + up_z(c))
    cell = lax.broadcasted_iota(jnp.int32, (CELLS, LANES), 0)
    not_last = lax.rem(cell, COLS) < COLS - 1
    face_x = jnp.where(not_last, 0.5 * (c + pltpu.roll(c, CELLS - 1, axis=0)), 0.0)

    def weighted(k, dy, dz, dx):
        fy = column(face_y, k) * dy
        fz = column(face_z, k) * dz
        fx = column(face_x, k) * dx
        net = fz - down_z(fz) + fx - pltpu.roll(fx, 1, axis=0)
        return net + jnp.concatenate([fy, -fy], axis=0)

    def diffs(x):
        return (
            x[:ROW_CELLS] - x[ROW_CELLS:],
            x - up_z(x),
            x - pltpu.roll(x, CELLS - 1, axis=0),
        )

    for t in range(WIDTH // LANES):
        lanes = slice(t * LANES, (t + 1) * LANES)
        x = u[:, lanes]
        center_ref[:, lanes] = weighted(0, *diffs(x))

    low_diffs = diffs(picked_ref[:, :LANES])
    low_sum = jnp.zeros((CELLS, LANES), F32)
    for k in range(1, variables + 1):
        out = slice((k - 1) * LANES, k * LANES)
        side_ref[:, out] = weighted(k, *low_diffs)
        level = level_ref[(k - 1) * 8 : (k - 1) * 8 + 1, :]
        low_sum = low_sum + level * weighted(k, *diffs(picked_ref[:, k * LANES : (k + 1) * LANES]))
    low_ref[...] = low_sum


def inner_shapes(turned_pairs):
    shape = jax.ShapeDtypeStruct
    variables = turned_pairs.shape[0]
    blocks = (variables + 1) * LANES
    return (
        shape((WIDTH, blocks), BF16),
        shape((blocks, WIDTH), BF16),
        shape((8 * variables, LANES), F32),
        shape((CELLS, variables * LANES), F32),
        shape((CELLS, LANES), F32),
        shape((CELLS, WIDTH), F32),
    )


def start(field, mean, kl, turned_pairs):
    shape = jax.ShapeDtypeStruct
    made = inner_shapes(turned_pairs)
    return pl.pallas_call(
        functools.partial(start_kernel, field.shape[-1]),
        out_shape=(
            shape((ROW_CELLS, WIDTH), F32),
            shape((ROW_CELLS, WIDTH), F32),
            shape((GROUPS, WIDTH), F32),
            shape((GROUPS, WIDTH), F32),
        )
        + made,
        in_specs=[HBM] * 4,
        out_specs=[IN_VMEM] * 10,
        scratch_shapes=[pltpu.VMEM(x.shape, x.dtype) for x in (field, mean, kl, turned_pairs)]
        + [pltpu.VMEM((CELLS, made[0].shape[1]), F32), pltpu.SemaphoreType.DMA((3,))],
        compiler_params=pltpu.CompilerParams(vmem_limit_bytes=44 * 1024 * 1024),
        name="start",
    )(field, mean, kl, turned_pairs)


def later(modes, low, high, turned_pairs):
    made = inner_shapes(turned_pairs)
    return pl.pallas_call(
        functools.partial(later_kernel, modes),
        out_shape=made,
        in_specs=[IN_VMEM, IN_VMEM, HBM],
        out_specs=[IN_VMEM] * 6,
        scratch_shapes=[
            pltpu.VMEM(turned_pairs.shape, turned_pairs.dtype),
            pltpu.VMEM((CELLS, made[0].shape[1]), F32),
            pltpu.SemaphoreType.DMA((1,)),
        ],
        compiler_params=pltpu.CompilerParams(vmem_limit_bytes=44 * 1024 * 1024),
        name="later",
    )(low, high, turned_pairs)


def outer_kernel(modes, *refs):
    rows, parts, parts_then = refs[:6], refs[6:12], refs[12:18]
    out_ref, terms_ref = refs[18:]
    for mine, given in ((early(), parts), (jnp.logical_not(early()), parts_then)):

        @pl.when(mine)
        def _(given=given):
            outer_body(modes, *rows, *given, out_ref, terms_ref)


def outer_body(modes, low_ref, high_ref, before_ref, behind_ref, left_ref, right_ref, pick_ref, place_ref, level_ref,
               side_ref, low_sum_ref, center_ref, out_ref, terms_ref):
    variables = side_ref.shape[1] // LANES
    own = jnp.concatenate([low_ref[...], high_ref[...]], axis=0)

    def strip(x):
        at = [g * COLS for g in range(GROUPS)] + [(g + 1) * COLS - 1 for g in range(GROUPS)]
        return jnp.concatenate([x[i : i + 1] for i in at], axis=0)

    def coefs(x):
        return x[:, WIDTH - LANES :]

    mine = jnp.concatenate([own, strip(own)], axis=0)
    theirs = jnp.concatenate([before_ref[...], behind_ref[...], left_ref[...], right_ref[...]], axis=0)
    lane = lax.broadcasted_iota(jnp.int32, mine.shape, 1)
    d = jnp.where(lane < modes, mine - theirs, 0.0)
    face = 0.5 * (coefs(mine) + coefs(theirs))
    row = lax.broadcasted_iota(jnp.int32, face.shape, 0)
    end = (lax.axis_index("wide") == 0) & (row < ROW_CELLS)
    end |= (lax.axis_index("narrow") == 0) & (row >= CELLS) & (row < CELLS + GROUPS)
    face = jnp.where(end, 0.0, face)
    count = face.shape[0]

    def with_own(ref, lanes, value):
        return jnp.concatenate([ref[:, lanes] + value[:CELLS], value[CELLS:]], axis=0)

    both = dot(split(d), pick_ref[...])
    picked = both[:count] + both[count:]
    low = picked[:, :LANES]
    low_sum = jnp.zeros_like(low)
    for k in range(1, variables + 1):
        level = level_ref[(k - 1) * 8 : (k - 1) * 8 + 1, :]
        f = column(face, k)
        low_sum = low_sum + level * (f * picked[:, k * LANES : (k + 1) * LANES])
        side = level * with_own(side_ref, slice((k - 1) * LANES, k * LANES), f * low)
        terms_ref[:, k * LANES : (k + 1) * LANES] = split(side)
    terms_ref[:, :LANES] = split(with_own(low_sum_ref, slice(0, LANES), low_sum))
    spread = dot(terms_ref[...], place_ref[...])
    f = column(face, 0)
    f = jnp.concatenate([f] * (WIDTH // LANES), axis=1)
    total = f * d + spread[:count] + spread[count:]
    inner_rows = center_ref[...] + total[:CELLS]
    for r in range(ROWS):
        out_ref[r] = inner_rows[r * ROW_CELLS : (r + 1) * ROW_CELLS, :modes]
    for g in range(GROUPS):
        r, z = divmod(g, DEPTH)
        for x, i in ((0, CELLS + g), (COLS - 1, CELLS + GROUPS + g)):
            out_ref[r, z * COLS + x : z * COLS + x + 1, :] += total[i : i + 1, :modes]


def outer(modes, low, high, before, behind, left, right, parts, parts_then):
    vmem = pl.BlockSpec(memory_space=pltpu.VMEM)
    blocks = parts[0].shape[1]
    edges = (low, high, before, behind, left, right)
    return pl.pallas_call(
        functools.partial(outer_kernel, modes),
        out_shape=jax.ShapeDtypeStruct((ROWS, ROW_CELLS, modes), F32),
        in_specs=[vmem] * 18,
        out_specs=vmem,
        scratch_shapes=[pltpu.VMEM((2 * (CELLS + 2 * GROUPS), blocks), BF16)],
        compiler_params=pltpu.CompilerParams(vmem_limit_bytes=40 * 1024 * 1024),
        name="outer",
    )(*edges, *parts, *parts_then)


def held(x):
    return pltpu.with_memory_space_constraint(x, pltpu.HBM)


def shift(block, axis, by):
    size = lax.axis_size(axis)
    route = [(i, i + by) for i in range(size) if 0 <= i + by < size]
    return lax.ppermute(block, axis, route)


RUNS = 4


def early():
    return lax.rem(lax.div(lax.axis_index("wide"), 2), RUNS) == 0


def per_device(chaos_field, mean_conductivity, kl_fields, pairs):
    modes = chaos_field.shape[-1]
    field = chaos_field.reshape(ROWS, ROW_CELLS, modes)
    turned = held(pairs.transpose(0, 2, 1))
    low, high, first, last, *parts = start(held(field), held(mean_conductivity), held(kl_fields), turned)
    before = shift(high, "wide", 1)
    behind = shift(low, "wide", -1)
    left = shift(last, "narrow", 1)
    right = shift(first, "narrow", -1)
    parts_then = later(modes, low, high, turned)
    out = outer(modes, low, high, before, behind, left, right, parts, parts_then)
    return out.reshape(chaos_field.shape)


def solution(mesh):
    placed = (
        P("wide", None, "narrow", None),
        P("wide", None, "narrow"),
        P(None, "wide", None, "narrow"),
        P(),
    )
    return jax.shard_map(
        per_device,
        mesh=mesh,
        in_specs=placed,
        out_specs=P("wide", None, "narrow", None),
        check_vma=False,
    )
```

```python
import functools

import jax
import jax.numpy as jnp
from jax import lax
from jax.experimental import pallas as pl
from jax.experimental.pallas import tpu as pltpu
from jax.sharding import PartitionSpec as P

F32, BF16 = jnp.float32, jnp.bfloat16
LANES = 128
ROWS, DEPTH, COLS = 2, 4, 16
ROW_CELLS = DEPTH * COLS
CELLS = ROWS * ROW_CELLS
GROUPS = ROWS * DEPTH
WIDTH = 512
HBM = pl.BlockSpec(memory_space=pltpu.HBM)
IN_VMEM = pl.BlockSpec(memory_space=pltpu.VMEM)
COEF = 72


def split(x):
    hi = x.astype(BF16)
    lo = (x - hi.astype(F32)).astype(BF16)
    return jnp.concatenate([hi, lo], axis=0)


def dot(a, b):
    return jnp.dot(a, b, preferred_element_type=F32)


def dot_t(a, b):
    return lax.dot_general(a, b, (((1,), (1,)), ((), ())), preferred_element_type=F32)


def fetch(sources, targets, sems):
    copies = [pltpu.make_async_copy(s, t, sems.at[i]) for i, (s, t) in enumerate(zip(sources, targets))]
    for copy in copies:
        copy.start()
    for copy in copies:
        copy.wait()


def pack_rows(modes, f_ref, mean_ref, kl_ref, low_ref, high_ref, sends, first_ref, last_ref):
    variables = kl_ref.shape[0]
    slabs = []
    for g in range(GROUPS):
        r, z = divmod(g, DEPTH)
        slabs.append(mean_ref[r, z : z + 1, :])
        slabs.append(kl_ref[:, r, z, :])
        slabs.append(jnp.zeros((COLS - 1 - variables, COLS), F32))
    stacked = jnp.concatenate(slabs, axis=0)
    stacked = jnp.concatenate([stacked, jnp.zeros((CELLS, LANES - COLS), F32)], axis=1)
    turned = stacked.T[:COLS]
    lane = lax.broadcasted_iota(jnp.int32, (COLS, LANES), 1)
    inside = (lane >= COEF) & (lane < COEF + variables + 1)
    behind = WIDTH - LANES
    for g in range(GROUPS):
        r, z = divmod(g, DEPTH)
        part = pltpu.roll(turned, (COEF - g * COLS) % LANES, axis=1)
        row = (low_ref, high_ref)[r]
        row[z * COLS : (z + 1) * COLS, behind:] = jnp.where(inside, part, 0.0)
    low_ref[:, :modes] = f_ref[0]
    high_ref[:, :modes] = f_ref[1]
    for up, ref in zip(goes_up(), sends):
        ref[...] = jnp.where(up, high_ref[...], low_ref[...])
    for g in range(GROUPS):
        r, z = divmod(g, DEPTH)
        row, at = (low_ref, high_ref)[r], z * COLS
        first_ref[g : g + 1, :] = row[at : at + 1, :]
        last_ref[g : g + 1, :] = row[at + COLS - 1 : at + COLS, :]


def modes_of(ref, modes):
    x = ref[...]
    lane = lax.broadcasted_iota(jnp.int32, x.shape, 1)
    return jnp.where(lane < modes, x, 0.0)


def coefs_of(ref):
    return ref[:, WIDTH - LANES :]


def column(coefs, k):
    return jnp.broadcast_to(coefs[:, COEF + k : COEF + k + 1], coefs.shape)


def tables(pairs_ref, pick_ref, place_ref, level_ref):
    variables, _, count = pairs_ref.shape
    mode = lax.broadcasted_iota(jnp.int32, (WIDTH, LANES), 0)
    lane = lax.broadcasted_iota(jnp.int32, (1, LANES), 1)
    used = lane < count

    def row(k, c):
        values = jnp.concatenate(
            [pairs_ref[k, c : c + 1, :], jnp.zeros((1, LANES - count), jnp.int32)], axis=1
        )
        return values

    low = jnp.where(used, row(0, 0), -1)
    low_column = jnp.broadcast_to(low, (LANES, LANES)).T
    eye = jnp.where(used & (low_column == low), 1.0, 0.0).astype(BF16)
    hot = jnp.where(mode == low, 1.0, 0.0).astype(BF16)
    pick_ref[:, :LANES] = hot
    place_ref[:LANES, :] = dot_t(eye, hot).astype(BF16)
    for k in range(variables):
        same = jnp.where(used & (low_column == row(k, 0)), 1.0, 0.0).astype(BF16)
        raised = jnp.where(mode == jnp.where(used, row(k, 1), -1), 1.0, 0.0).astype(BF16)
        levels = jnp.broadcast_to(jnp.where(used, row(k, 2), 0).astype(F32), (16, LANES)).astype(BF16)
        at = (k + 1) * LANES
        pick_ref[:, at : at + LANES] = dot_t(raised, same).astype(BF16)
        place_ref[at : at + LANES, :] = dot_t(same, raised).astype(BF16)
        level_ref[k * 8 : (k + 1) * 8, :] = jnp.sqrt(dot_t(levels, same)[:8])


def start_kernel(modes, f_hbm, mean_hbm, kl_hbm, pairs_hbm, low_ref, high_ref, *refs):
    sends, (first_ref, last_ref), given = refs[:3], refs[3:5], refs[5:11]
    f_ref, mean_ref, kl_ref, pairs_ref, picked_ref, sems = refs[11:]
    fetch((f_hbm, mean_hbm, kl_hbm), (f_ref, mean_ref, kl_ref), sems)
    pack_rows(modes, f_ref, mean_ref, kl_ref, low_ref, high_ref, sends, first_ref, last_ref)

    @pl.when(early())
    def _():
        fetch((pairs_hbm,), (pairs_ref,), sems)
        inner(modes, low_ref, high_ref, pairs_ref, *given, picked_ref)


def later_kernel(modes, low_ref, high_ref, pairs_hbm, *refs):
    given, (pairs_ref, picked_ref, sems) = refs[:6], refs[6:]

    @pl.when(jnp.logical_not(early()))
    def _():
        fetch((pairs_hbm,), (pairs_ref,), sems)
        inner(modes, low_ref, high_ref, pairs_ref, *given, picked_ref)


def inner(modes, a_ref, b_ref, pairs_ref, pick_ref, place_ref, level_ref, side_ref, low_ref, center_ref, picked_ref):
    variables = pairs_ref.shape[0]
    tables(pairs_ref, pick_ref, place_ref, level_ref)

    u = jnp.concatenate([modes_of(a_ref, modes), modes_of(b_ref, modes)], axis=0)
    c = jnp.concatenate([coefs_of(a_ref), coefs_of(b_ref)], axis=0)
    both = dot(split(u), pick_ref[...])
    picked_ref[...] = both[:CELLS] + both[CELLS:]

    face_y = 0.5 * (c[:ROW_CELLS] + c[ROW_CELLS:])
    zero = jnp.zeros((COLS, LANES), F32)

    def up_z(x):
        return jnp.concatenate(
            [x[COLS:ROW_CELLS], zero, x[ROW_CELLS + COLS :], zero], axis=0
        )

    def down_z(x):
        return jnp.concatenate(
            [zero, x[: ROW_CELLS - COLS], zero, x[ROW_CELLS : CELLS - COLS]], axis=0
        )

    face_z = 0.5 * (c + up_z(c))
    cell = lax.broadcasted_iota(jnp.int32, (CELLS, LANES), 0)
    not_last = lax.rem(cell, COLS) < COLS - 1
    face_x = jnp.where(not_last, 0.5 * (c + pltpu.roll(c, CELLS - 1, axis=0)), 0.0)

    def weighted(k, dy, dz, dx):
        fy = column(face_y, k) * dy
        fz = column(face_z, k) * dz
        fx = column(face_x, k) * dx
        net = fz - down_z(fz) + fx - pltpu.roll(fx, 1, axis=0)
        return net + jnp.concatenate([fy, -fy], axis=0)

    def diffs(x):
        return (
            x[:ROW_CELLS] - x[ROW_CELLS:],
            x - up_z(x),
            x - pltpu.roll(x, CELLS - 1, axis=0),
        )

    for t in range(WIDTH // LANES):
        lanes = slice(t * LANES, (t + 1) * LANES)
        x = u[:, lanes]
        center_ref[:, lanes] = weighted(0, *diffs(x))

    low_diffs = diffs(picked_ref[:, :LANES])
    low_sum = jnp.zeros((CELLS, LANES), F32)
    for k in range(1, variables + 1):
        out = slice((k - 1) * LANES, k * LANES)
        side_ref[:, out] = weighted(k, *low_diffs)
        level = level_ref[(k - 1) * 8 : (k - 1) * 8 + 1, :]
        low_sum = low_sum + level * weighted(k, *diffs(picked_ref[:, k * LANES : (k + 1) * LANES]))
    low_ref[...] = low_sum


def inner_shapes(turned_pairs):
    shape = jax.ShapeDtypeStruct
    variables = turned_pairs.shape[0]
    blocks = (variables + 1) * LANES
    return (
        shape((WIDTH, blocks), BF16),
        shape((blocks, WIDTH), BF16),
        shape((8 * variables, LANES), F32),
        shape((CELLS, variables * LANES), F32),
        shape((CELLS, LANES), F32),
        shape((CELLS, WIDTH), F32),
    )


def start(field, mean, kl, turned_pairs):
    shape = jax.ShapeDtypeStruct
    made = inner_shapes(turned_pairs)
    return pl.pallas_call(
        functools.partial(start_kernel, field.shape[-1]),
        out_shape=(shape((ROW_CELLS, WIDTH), F32),) * 5 + (shape((GROUPS, WIDTH), F32),) * 2 + made,
        in_specs=[HBM] * 4,
        out_specs=[IN_VMEM] * 13,
        scratch_shapes=[pltpu.VMEM(x.shape, x.dtype) for x in (field, mean, kl, turned_pairs)]
        + [pltpu.VMEM((CELLS, made[0].shape[1]), F32), pltpu.SemaphoreType.DMA((3,))],
        compiler_params=pltpu.CompilerParams(vmem_limit_bytes=44 * 1024 * 1024),
        name="start",
    )(field, mean, kl, turned_pairs)


def later(modes, low, high, turned_pairs):
    made = inner_shapes(turned_pairs)
    return pl.pallas_call(
        functools.partial(later_kernel, modes),
        out_shape=made,
        in_specs=[IN_VMEM, IN_VMEM, HBM],
        out_specs=[IN_VMEM] * 6,
        scratch_shapes=[
            pltpu.VMEM(turned_pairs.shape, turned_pairs.dtype),
            pltpu.VMEM((CELLS, made[0].shape[1]), F32),
            pltpu.SemaphoreType.DMA((1,)),
        ],
        compiler_params=pltpu.CompilerParams(vmem_limit_bytes=44 * 1024 * 1024),
        name="later",
    )(low, high, turned_pairs)


def outer_kernel(modes, *refs):
    rows, parts, parts_then = refs[:9], refs[9:15], refs[15:21]
    out_ref, terms_ref = refs[21:]
    for mine, given in ((early(), parts), (jnp.logical_not(early()), parts_then)):

        @pl.when(mine)
        def _(given=given):
            outer_body(modes, *rows, *given, out_ref, terms_ref)


def outer_body(modes, low_ref, high_ref, rows1_ref, rows2_ref, rows3_ref, left_ref, right_ref, left_then_ref,
               right_then_ref, pick_ref, place_ref, level_ref, side_ref, low_sum_ref, center_ref,
               out_ref, terms_ref):
    variables = side_ref.shape[1] // LANES
    own = jnp.concatenate([low_ref[...], high_ref[...]], axis=0)

    def strip(x):
        at = [g * COLS for g in range(GROUPS)] + [(g + 1) * COLS - 1 for g in range(GROUPS)]
        return jnp.concatenate([x[i : i + 1] for i in at], axis=0)

    def coefs(x):
        return x[:, WIDTH - LANES :]

    mine = jnp.concatenate([own, strip(own)], axis=0)
    given = (rows1_ref[...], rows2_ref[...], rows3_ref[...])
    before, behind = (pick_from(given, which) for which in comes_in())
    left = jnp.where(early(), left_ref[...], left_then_ref[...])
    right = jnp.where(early(), right_ref[...], right_then_ref[...])
    theirs = jnp.concatenate([before, behind, left, right], axis=0)
    lane = lax.broadcasted_iota(jnp.int32, mine.shape, 1)
    d = jnp.where(lane < modes, mine - theirs, 0.0)
    face = 0.5 * (coefs(mine) + coefs(theirs))
    row = lax.broadcasted_iota(jnp.int32, face.shape, 0)
    end = (lax.axis_index("wide") == 0) & (row < ROW_CELLS)
    end |= (lax.axis_index("narrow") == 0) & (row >= CELLS) & (row < CELLS + GROUPS)
    face = jnp.where(end, 0.0, face)
    count = face.shape[0]

    def with_own(ref, lanes, value):
        return jnp.concatenate([ref[:, lanes] + value[:CELLS], value[CELLS:]], axis=0)

    both = dot(split(d), pick_ref[...])
    picked = both[:count] + both[count:]
    low = picked[:, :LANES]
    low_sum = jnp.zeros_like(low)
    for k in range(1, variables + 1):
        level = level_ref[(k - 1) * 8 : (k - 1) * 8 + 1, :]
        f = column(face, k)
        low_sum = low_sum + level * (f * picked[:, k * LANES : (k + 1) * LANES])
        side = level * with_own(side_ref, slice((k - 1) * LANES, k * LANES), f * low)
        terms_ref[:, k * LANES : (k + 1) * LANES] = split(side)
    terms_ref[:, :LANES] = split(with_own(low_sum_ref, slice(0, LANES), low_sum))
    spread = dot(terms_ref[...], place_ref[...])
    f = column(face, 0)
    f = jnp.concatenate([f] * (WIDTH // LANES), axis=1)
    total = f * d + spread[:count] + spread[count:]
    inner_rows = center_ref[...] + total[:CELLS]
    for r in range(ROWS):
        out_ref[r] = inner_rows[r * ROW_CELLS : (r + 1) * ROW_CELLS, :modes]
    for g in range(GROUPS):
        r, z = divmod(g, DEPTH)
        for x, i in ((0, CELLS + g), (COLS - 1, CELLS + GROUPS + g)):
            out_ref[r, z * COLS + x : z * COLS + x + 1, :] += total[i : i + 1, :modes]


def outer(modes, low, high, rows, columns, parts, parts_then):
    vmem = pl.BlockSpec(memory_space=pltpu.VMEM)
    blocks = parts[0].shape[1]
    edges = (low, high, *rows, *columns)
    return pl.pallas_call(
        functools.partial(outer_kernel, modes),
        out_shape=jax.ShapeDtypeStruct((ROWS, ROW_CELLS, modes), F32),
        in_specs=[vmem] * 21,
        out_specs=vmem,
        scratch_shapes=[pltpu.VMEM((2 * (CELLS + 2 * GROUPS), blocks), BF16)],
        compiler_params=pltpu.CompilerParams(vmem_limit_bytes=40 * 1024 * 1024),
        name="outer",
    )(*edges, *parts, *parts_then)


def held(x):
    return pltpu.with_memory_space_constraint(x, pltpu.HBM)


RUN = 8
LAST = RUN - 1


def early():
    return lax.rem(lax.axis_index("wide"), RUN) < 2


def goes_up():
    at = lax.rem(lax.axis_index("wide"), RUN)
    return at == LAST, (at == 0) | (at == LAST - 1), at > 0


def comes_in():
    at = lax.rem(lax.axis_index("wide"), RUN)
    before = jnp.where(at == 0, 0, jnp.where((at == 1) | (at == LAST), 1, 2))
    behind = jnp.where(at == LAST, 2, jnp.where((at == 0) | (at == LAST - 1), 1, 0))
    return before, behind


def pick_from(given, which):
    return jnp.where(which == 0, given[0], jnp.where(which == 1, given[1], given[2]))


def steps(turn, at):
    if turn == 0:
        return 1 if at == LAST else -1 if at >= 2 else 0
    if turn == 1:
        return {0: 1, 1: -1, LAST - 1: 1, LAST: -1}.get(at, 0)
    return -1 if at == 0 else 1 if at <= LAST - 2 else 0


def send_rows(block, turn):
    size = lax.axis_size("wide")
    route = [(i, i + steps(turn, i % RUN)) for i in range(size) if steps(turn, i % RUN)]
    return lax.ppermute(block, "wide", [(i, j) for i, j in route if 0 <= j < size])


def send_columns(block, by, is_early):
    wide, narrow = lax.axis_size("wide"), lax.axis_size("narrow")
    route = [
        (w * narrow + n, w * narrow + n + by)
        for w in range(wide)
        for n in range(narrow)
        if (w % RUN < 2) == is_early and 0 <= n + by < narrow
    ]
    return lax.ppermute(block, ("wide", "narrow"), route)


def per_device(chaos_field, mean_conductivity, kl_fields, pairs):
    modes = chaos_field.shape[-1]
    field = chaos_field.reshape(ROWS, ROW_CELLS, modes)
    turned = held(pairs.transpose(0, 2, 1))
    low, high, send1, send2, send3, first, last, *parts = start(
        held(field), held(mean_conductivity), held(kl_fields), turned
    )
    rows1 = send_rows(send1, 0)
    left = send_columns(last, 1, True)
    right = send_columns(first, -1, True)
    rows2 = send_rows(send2, 1)
    send3, left, right = lax.optimization_barrier((send3, left, right))
    rows3 = send_rows(send3, 2)
    left_then = send_columns(last, 1, False)
    right_then = send_columns(first, -1, False)
    parts_then = later(modes, low, high, turned)
    columns = (left, right, left_then, right_then)
    out = outer(modes, low, high, (rows1, rows2, rows3), columns, parts, parts_then)
    return out.reshape(chaos_field.shape)


def solution(mesh):
    placed = (
        P("wide", None, "narrow", None),
        P("wide", None, "narrow"),
        P(None, "wide", None, "narrow"),
        P(),
    )
    return jax.shard_map(
        per_device,
        mesh=mesh,
        in_specs=placed,
        out_specs=P("wide", None, "narrow", None),
        check_vma=False,
    )
```

```python
import functools

import jax
import jax.numpy as jnp
from jax import lax
from jax.experimental import pallas as pl
from jax.experimental.pallas import tpu as pltpu
from jax.sharding import PartitionSpec as P

F32, BF16 = jnp.float32, jnp.bfloat16
LANES = 128
ROWS, DEPTH, COLS = 2, 4, 16
ROW_CELLS = DEPTH * COLS
CELLS = ROWS * ROW_CELLS
GROUPS = ROWS * DEPTH
WIDTH = 512
HBM = pl.BlockSpec(memory_space=pltpu.HBM)
IN_VMEM = pl.BlockSpec(memory_space=pltpu.VMEM)
COEF = 72


def split(x):
    hi = x.astype(BF16)
    lo = (x - hi.astype(F32)).astype(BF16)
    return jnp.concatenate([hi, lo], axis=0)


def dot(a, b):
    return jnp.dot(a, b, preferred_element_type=F32)


def dot_t(a, b):
    return lax.dot_general(a, b, (((1,), (1,)), ((), ())), preferred_element_type=F32)


def fetch(sources, targets, sems):
    copies = [pltpu.make_async_copy(s, t, sems.at[i]) for i, (s, t) in enumerate(zip(sources, targets))]
    for copy in copies:
        copy.start()
    for copy in copies:
        copy.wait()


def pack_rows(modes, f_ref, mean_ref, kl_ref, low_ref, high_ref, sends, first_ref, last_ref):
    variables = kl_ref.shape[0]
    slabs = []
    for g in range(GROUPS):
        r, z = divmod(g, DEPTH)
        slabs.append(mean_ref[r, z : z + 1, :])
        slabs.append(kl_ref[:, r, z, :])
        slabs.append(jnp.zeros((COLS - 1 - variables, COLS), F32))
    stacked = jnp.concatenate(slabs, axis=0)
    stacked = jnp.concatenate([stacked, jnp.zeros((CELLS, LANES - COLS), F32)], axis=1)
    turned = stacked.T[:COLS]
    lane = lax.broadcasted_iota(jnp.int32, (COLS, LANES), 1)
    inside = (lane >= COEF) & (lane < COEF + variables + 1)
    behind = WIDTH - LANES
    for g in range(GROUPS):
        r, z = divmod(g, DEPTH)
        part = pltpu.roll(turned, (COEF - g * COLS) % LANES, axis=1)
        row = (low_ref, high_ref)[r]
        row[z * COLS : (z + 1) * COLS, behind:] = jnp.where(inside, part, 0.0)
    low_ref[:, :modes] = f_ref[0]
    high_ref[:, :modes] = f_ref[1]
    for up, ref in zip(goes_up(), sends):
        ref[...] = jnp.where(up, high_ref[...], low_ref[...])
    for g in range(GROUPS):
        r, z = divmod(g, DEPTH)
        row, at = (low_ref, high_ref)[r], z * COLS
        first_ref[g : g + 1, :] = row[at : at + 1, :]
        last_ref[g : g + 1, :] = row[at + COLS - 1 : at + COLS, :]


def modes_of(ref, modes):
    x = ref[...]
    lane = lax.broadcasted_iota(jnp.int32, x.shape, 1)
    return jnp.where(lane < modes, x, 0.0)


def coefs_of(ref):
    return ref[:, WIDTH - LANES :]


def column(coefs, k):
    return jnp.broadcast_to(coefs[:, COEF + k : COEF + k + 1], coefs.shape)


def tables(pairs_ref, pick_ref, place_ref, level_ref):
    variables, _, count = pairs_ref.shape
    mode = lax.broadcasted_iota(jnp.int32, (WIDTH, LANES), 0)
    lane = lax.broadcasted_iota(jnp.int32, (1, LANES), 1)
    used = lane < count

    def row(k, c):
        values = jnp.concatenate(
            [pairs_ref[k, c : c + 1, :], jnp.zeros((1, LANES - count), jnp.int32)], axis=1
        )
        return values

    low = jnp.where(used, row(0, 0), -1)
    low_column = jnp.broadcast_to(low, (LANES, LANES)).T
    eye = jnp.where(used & (low_column == low), 1.0, 0.0).astype(BF16)
    hot = jnp.where(mode == low, 1.0, 0.0).astype(BF16)
    pick_ref[:, :LANES] = hot
    place_ref[:LANES, :] = dot_t(eye, hot).astype(BF16)
    for k in range(variables):
        same = jnp.where(used & (low_column == row(k, 0)), 1.0, 0.0).astype(BF16)
        raised = jnp.where(mode == jnp.where(used, row(k, 1), -1), 1.0, 0.0).astype(BF16)
        levels = jnp.broadcast_to(jnp.where(used, row(k, 2), 0).astype(F32), (16, LANES)).astype(BF16)
        at = (k + 1) * LANES
        pick_ref[:, at : at + LANES] = dot_t(raised, same).astype(BF16)
        place_ref[at : at + LANES, :] = dot_t(same, raised).astype(BF16)
        level_ref[k * 8 : (k + 1) * 8, :] = jnp.sqrt(dot_t(levels, same)[:8])


def pack_kernel(modes, f_hbm, mean_hbm, kl_hbm, low_ref, high_ref, *refs):
    sends, (first_ref, last_ref), (f_ref, mean_ref, kl_ref, sems) = refs[:3], refs[3:5], refs[5:]
    fetch((f_hbm, mean_hbm, kl_hbm), (f_ref, mean_ref, kl_ref), sems)
    pack_rows(modes, f_ref, mean_ref, kl_ref, low_ref, high_ref, sends, first_ref, last_ref)


def first_kernel(modes, passed, low_ref, high_ref, pairs_hbm, *refs):
    given, (pairs_ref, picked_ref, sems) = refs[passed : passed + 6], refs[2 * passed + 6 :]

    @pl.when(early())
    def _():
        fetch((pairs_hbm,), (pairs_ref,), sems)
        inner(modes, low_ref, high_ref, pairs_ref, *given, picked_ref)


def later_kernel(modes, low_ref, high_ref, pairs_hbm, *refs):
    given, (pairs_ref, picked_ref, sems) = refs[:6], refs[6:]

    @pl.when(jnp.logical_not(early()))
    def _():
        fetch((pairs_hbm,), (pairs_ref,), sems)
        inner(modes, low_ref, high_ref, pairs_ref, *given, picked_ref)


def inner(modes, a_ref, b_ref, pairs_ref, pick_ref, place_ref, level_ref, side_ref, low_ref, center_ref, picked_ref):
    variables = pairs_ref.shape[0]
    tables(pairs_ref, pick_ref, place_ref, level_ref)

    u = jnp.concatenate([modes_of(a_ref, modes), modes_of(b_ref, modes)], axis=0)
    c = jnp.concatenate([coefs_of(a_ref), coefs_of(b_ref)], axis=0)
    both = dot(split(u), pick_ref[...])
    picked_ref[...] = both[:CELLS] + both[CELLS:]

    face_y = 0.5 * (c[:ROW_CELLS] + c[ROW_CELLS:])
    zero = jnp.zeros((COLS, LANES), F32)

    def up_z(x):
        return jnp.concatenate(
            [x[COLS:ROW_CELLS], zero, x[ROW_CELLS + COLS :], zero], axis=0
        )

    def down_z(x):
        return jnp.concatenate(
            [zero, x[: ROW_CELLS - COLS], zero, x[ROW_CELLS : CELLS - COLS]], axis=0
        )

    face_z = 0.5 * (c + up_z(c))
    cell = lax.broadcasted_iota(jnp.int32, (CELLS, LANES), 0)
    not_last = lax.rem(cell, COLS) < COLS - 1
    face_x = jnp.where(not_last, 0.5 * (c + pltpu.roll(c, CELLS - 1, axis=0)), 0.0)

    def weighted(k, dy, dz, dx):
        fy = column(face_y, k) * dy
        fz = column(face_z, k) * dz
        fx = column(face_x, k) * dx
        net = fz - down_z(fz) + fx - pltpu.roll(fx, 1, axis=0)
        return net + jnp.concatenate([fy, -fy], axis=0)

    def diffs(x):
        return (
            x[:ROW_CELLS] - x[ROW_CELLS:],
            x - up_z(x),
            x - pltpu.roll(x, CELLS - 1, axis=0),
        )

    for t in range(WIDTH // LANES):
        lanes = slice(t * LANES, (t + 1) * LANES)
        x = u[:, lanes]
        center_ref[:, lanes] = weighted(0, *diffs(x))

    low_diffs = diffs(picked_ref[:, :LANES])
    low_sum = jnp.zeros((CELLS, LANES), F32)
    for k in range(1, variables + 1):
        out = slice((k - 1) * LANES, k * LANES)
        side_ref[:, out] = weighted(k, *low_diffs)
        level = level_ref[(k - 1) * 8 : (k - 1) * 8 + 1, :]
        low_sum = low_sum + level * weighted(k, *diffs(picked_ref[:, k * LANES : (k + 1) * LANES]))
    low_ref[...] = low_sum


def inner_shapes(turned_pairs):
    shape = jax.ShapeDtypeStruct
    variables = turned_pairs.shape[0]
    blocks = (variables + 1) * LANES
    return (
        shape((WIDTH, blocks), BF16),
        shape((blocks, WIDTH), BF16),
        shape((8 * variables, LANES), F32),
        shape((CELLS, variables * LANES), F32),
        shape((CELLS, LANES), F32),
        shape((CELLS, WIDTH), F32),
    )


def pack(field, mean, kl):
    shape = jax.ShapeDtypeStruct
    return pl.pallas_call(
        functools.partial(pack_kernel, field.shape[-1]),
        out_shape=(shape((ROW_CELLS, WIDTH), F32),) * 5 + (shape((GROUPS, WIDTH), F32),) * 2,
        in_specs=[HBM] * 3,
        out_specs=[IN_VMEM] * 7,
        scratch_shapes=[pltpu.VMEM(x.shape, x.dtype) for x in (field, mean, kl)] + [pltpu.SemaphoreType.DMA((3,))],
        compiler_params=pltpu.CompilerParams(vmem_limit_bytes=44 * 1024 * 1024),
        name="pack",
    )(field, mean, kl)


def inner_scratch(turned_pairs, made):
    return [
        pltpu.VMEM(turned_pairs.shape, turned_pairs.dtype),
        pltpu.VMEM((CELLS, made[0].shape[1]), F32),
        pltpu.SemaphoreType.DMA((1,)),
    ]


def first_work(modes, low, high, turned_pairs, sends):
    made = inner_shapes(turned_pairs)
    anywhere = pl.BlockSpec(memory_space=pl.ANY)
    out = pl.pallas_call(
        functools.partial(first_kernel, modes, len(sends)),
        out_shape=made + tuple(jax.ShapeDtypeStruct(x.shape, x.dtype) for x in sends),
        in_specs=[IN_VMEM, IN_VMEM, HBM] + [anywhere] * len(sends),
        out_specs=[IN_VMEM] * 6 + [anywhere] * len(sends),
        scratch_shapes=inner_scratch(turned_pairs, made),
        input_output_aliases={3 + i: 6 + i for i in range(len(sends))},
        compiler_params=pltpu.CompilerParams(vmem_limit_bytes=44 * 1024 * 1024),
        name="first_work",
    )(low, high, turned_pairs, *sends)
    return out[:6], out[6:]


def later(modes, low, high, turned_pairs):
    made = inner_shapes(turned_pairs)
    return pl.pallas_call(
        functools.partial(later_kernel, modes),
        out_shape=made,
        in_specs=[IN_VMEM, IN_VMEM, HBM],
        out_specs=[IN_VMEM] * 6,
        scratch_shapes=inner_scratch(turned_pairs, made),
        compiler_params=pltpu.CompilerParams(vmem_limit_bytes=44 * 1024 * 1024),
        name="later",
    )(low, high, turned_pairs)


def outer_kernel(modes, *refs):
    rows, parts, parts_then = refs[:9], refs[9:15], refs[15:21]
    out_ref, terms_ref = refs[21:]
    for mine, given in ((early(), parts), (jnp.logical_not(early()), parts_then)):

        @pl.when(mine)
        def _(given=given):
            outer_body(modes, *rows, *given, out_ref, terms_ref)


def outer_body(modes, low_ref, high_ref, rows1_ref, rows2_ref, rows3_ref, left_ref, right_ref, left_then_ref,
               right_then_ref, pick_ref, place_ref, level_ref, side_ref, low_sum_ref, center_ref,
               out_ref, terms_ref):
    variables = side_ref.shape[1] // LANES
    own = jnp.concatenate([low_ref[...], high_ref[...]], axis=0)

    def strip(x):
        at = [g * COLS for g in range(GROUPS)] + [(g + 1) * COLS - 1 for g in range(GROUPS)]
        return jnp.concatenate([x[i : i + 1] for i in at], axis=0)

    def coefs(x):
        return x[:, WIDTH - LANES :]

    mine = jnp.concatenate([own, strip(own)], axis=0)
    given = (rows1_ref[...], rows2_ref[...], rows3_ref[...])
    before, behind = (pick_from(given, which) for which in comes_in())
    left = jnp.where(early(), left_ref[...], left_then_ref[...])
    right = jnp.where(early(), right_ref[...], right_then_ref[...])
    theirs = jnp.concatenate([before, behind, left, right], axis=0)
    lane = lax.broadcasted_iota(jnp.int32, mine.shape, 1)
    d = jnp.where(lane < modes, mine - theirs, 0.0)
    face = 0.5 * (coefs(mine) + coefs(theirs))
    row = lax.broadcasted_iota(jnp.int32, face.shape, 0)
    end = (lax.axis_index("wide") == 0) & (row < ROW_CELLS)
    end |= (lax.axis_index("narrow") == 0) & (row >= CELLS) & (row < CELLS + GROUPS)
    face = jnp.where(end, 0.0, face)
    count = face.shape[0]

    def with_own(ref, lanes, value):
        return jnp.concatenate([ref[:, lanes] + value[:CELLS], value[CELLS:]], axis=0)

    both = dot(split(d), pick_ref[...])
    picked = both[:count] + both[count:]
    low = picked[:, :LANES]
    low_sum = jnp.zeros_like(low)
    for k in range(1, variables + 1):
        level = level_ref[(k - 1) * 8 : (k - 1) * 8 + 1, :]
        f = column(face, k)
        low_sum = low_sum + level * (f * picked[:, k * LANES : (k + 1) * LANES])
        side = level * with_own(side_ref, slice((k - 1) * LANES, k * LANES), f * low)
        terms_ref[:, k * LANES : (k + 1) * LANES] = split(side)
    terms_ref[:, :LANES] = split(with_own(low_sum_ref, slice(0, LANES), low_sum))
    spread = dot(terms_ref[...], place_ref[...])
    f = column(face, 0)
    f = jnp.concatenate([f] * (WIDTH // LANES), axis=1)
    total = f * d + spread[:count] + spread[count:]
    inner_rows = center_ref[...] + total[:CELLS]
    for r in range(ROWS):
        out_ref[r] = inner_rows[r * ROW_CELLS : (r + 1) * ROW_CELLS, :modes]
    for g in range(GROUPS):
        r, z = divmod(g, DEPTH)
        for x, i in ((0, CELLS + g), (COLS - 1, CELLS + GROUPS + g)):
            out_ref[r, z * COLS + x : z * COLS + x + 1, :] += total[i : i + 1, :modes]


def outer(modes, low, high, rows, columns, parts, parts_then):
    vmem = pl.BlockSpec(memory_space=pltpu.VMEM)
    blocks = parts[0].shape[1]
    edges = (low, high, *rows, *columns)
    return pl.pallas_call(
        functools.partial(outer_kernel, modes),
        out_shape=jax.ShapeDtypeStruct((ROWS, ROW_CELLS, modes), F32),
        in_specs=[vmem] * 21,
        out_specs=vmem,
        scratch_shapes=[pltpu.VMEM((2 * (CELLS + 2 * GROUPS), blocks), BF16)],
        compiler_params=pltpu.CompilerParams(vmem_limit_bytes=40 * 1024 * 1024),
        name="outer",
    )(*edges, *parts, *parts_then)


def held(x):
    return pltpu.with_memory_space_constraint(x, pltpu.HBM)


RUN = 8
LAST = RUN - 1


def early():
    return lax.rem(lax.axis_index("wide"), RUN) < 2


def goes_up():
    at = lax.rem(lax.axis_index("wide"), RUN)
    return at == LAST, at != 1, (at > 0) & (at < LAST)


def comes_in():
    at = lax.rem(lax.axis_index("wide"), RUN)
    before = jnp.where(at == 0, 0, jnp.where((at == 1) | (at >= LAST - 1), 1, 2))
    behind = jnp.where(at >= LAST - 1, 2, jnp.where(at == 0, 1, 0))
    return before, behind


def pick_from(given, which):
    return jnp.where(which == 0, given[0], jnp.where(which == 1, given[1], given[2]))


def steps(turn, at):
    if turn == 0:
        return 1 if at == LAST else -1 if at >= 2 else 0
    if turn == 1:
        return {0: 1, 1: -1, LAST - 2: 1, LAST - 1: 1}.get(at, 0)
    return -1 if at in (0, LAST) else 1 if at < LAST - 2 else 0


def send_rows(block, turn):
    size = lax.axis_size("wide")
    route = [(i, i + steps(turn, i % RUN)) for i in range(size) if steps(turn, i % RUN)]
    return lax.ppermute(block, "wide", [(i, j) for i, j in route if 0 <= j < size])


def send_columns(block, by, is_early):
    wide, narrow = lax.axis_size("wide"), lax.axis_size("narrow")
    route = [
        (w * narrow + n, w * narrow + n + by)
        for w in range(wide)
        for n in range(narrow)
        if (w % RUN < 2) == is_early and 0 <= n + by < narrow
    ]
    return lax.ppermute(block, ("wide", "narrow"), route)


def per_device(chaos_field, mean_conductivity, kl_fields, pairs):
    modes = chaos_field.shape[-1]
    field = chaos_field.reshape(ROWS, ROW_CELLS, modes)
    turned = held(pairs.transpose(0, 2, 1))
    low, high, send1, send2, send3, first, last = pack(held(field), held(mean_conductivity), held(kl_fields))
    rows1 = send_rows(send1, 0)
    parts, (send2, send3, first, last) = first_work(modes, low, high, turned, (send2, send3, first, last))
    left = send_columns(last, 1, True)
    right = send_columns(first, -1, True)
    rows2 = send_rows(send2, 1)
    send3, left, right, rows1 = lax.optimization_barrier((send3, left, right, rows1))
    rows3 = send_rows(send3, 2)
    left_then = send_columns(last, 1, False)
    right_then = send_columns(first, -1, False)
    parts_then = later(modes, low, high, turned)
    columns = (left, right, left_then, right_then)
    out = outer(modes, low, high, (rows1, rows2, rows3), columns, parts, parts_then)
    return out.reshape(chaos_field.shape)


def solution(mesh):
    placed = (
        P("wide", None, "narrow", None),
        P("wide", None, "narrow"),
        P(None, "wide", None, "narrow"),
        P(),
    )
    return jax.shard_map(
        per_device,
        mesh=mesh,
        in_specs=placed,
        out_specs=P("wide", None, "narrow", None),
        check_vma=False,
    )
```

```python
import functools

import jax
import jax.numpy as jnp
from jax import lax
from jax.experimental import pallas as pl
from jax.experimental.pallas import tpu as pltpu
from jax.sharding import PartitionSpec as P

F32, BF16 = jnp.float32, jnp.bfloat16
LANES = 128
ROWS, DEPTH, COLS = 2, 4, 16
ROW_CELLS = DEPTH * COLS
CELLS = ROWS * ROW_CELLS
GROUPS = ROWS * DEPTH
WIDTH = 512
HBM = pl.BlockSpec(memory_space=pltpu.HBM)
IN_VMEM = pl.BlockSpec(memory_space=pltpu.VMEM)
COEF = 72


def split(x):
    hi = x.astype(BF16)
    lo = (x - hi.astype(F32)).astype(BF16)
    return jnp.concatenate([hi, lo], axis=0)


def dot(a, b):
    return jnp.dot(a, b, preferred_element_type=F32)


def dot_t(a, b):
    return lax.dot_general(a, b, (((1,), (1,)), ((), ())), preferred_element_type=F32)


def fetch(sources, targets, sems):
    copies = [pltpu.make_async_copy(s, t, sems.at[i]) for i, (s, t) in enumerate(zip(sources, targets))]
    for copy in copies:
        copy.start()
    for copy in copies:
        copy.wait()


def pack_rows(modes, f_ref, mean_ref, kl_ref, low_ref, high_ref, sends, first_ref, last_ref):
    variables = kl_ref.shape[0]
    slabs = []
    for g in range(GROUPS):
        r, z = divmod(g, DEPTH)
        slabs.append(mean_ref[r, z : z + 1, :])
        slabs.append(kl_ref[:, r, z, :])
        slabs.append(jnp.zeros((COLS - 1 - variables, COLS), F32))
    stacked = jnp.concatenate(slabs, axis=0)
    stacked = jnp.concatenate([stacked, jnp.zeros((CELLS, LANES - COLS), F32)], axis=1)
    turned = stacked.T[:COLS]
    lane = lax.broadcasted_iota(jnp.int32, (COLS, LANES), 1)
    inside = (lane >= COEF) & (lane < COEF + variables + 1)
    behind = WIDTH - LANES
    for g in range(GROUPS):
        r, z = divmod(g, DEPTH)
        part = pltpu.roll(turned, (COEF - g * COLS) % LANES, axis=1)
        row = (low_ref, high_ref)[r]
        row[z * COLS : (z + 1) * COLS, behind:] = jnp.where(inside, part, 0.0)
    low_ref[:, :modes] = f_ref[0]
    high_ref[:, :modes] = f_ref[1]
    for up, ref in zip(goes_up(), sends):
        ref[...] = jnp.where(up, high_ref[...], low_ref[...])
    for g in range(GROUPS):
        r, z = divmod(g, DEPTH)
        row, at = (low_ref, high_ref)[r], z * COLS
        first_ref[g : g + 1, :] = row[at : at + 1, :]
        last_ref[g : g + 1, :] = row[at + COLS - 1 : at + COLS, :]


def modes_of(ref, modes):
    x = ref[...]
    lane = lax.broadcasted_iota(jnp.int32, x.shape, 1)
    return jnp.where(lane < modes, x, 0.0)


def coefs_of(ref):
    return ref[:, WIDTH - LANES :]


def column(coefs, k):
    return jnp.broadcast_to(coefs[:, COEF + k : COEF + k + 1], coefs.shape)


def tables(pairs_ref, pick_ref, place_ref, level_ref):
    variables, _, count = pairs_ref.shape
    mode = lax.broadcasted_iota(jnp.int32, (WIDTH, LANES), 0)
    lane = lax.broadcasted_iota(jnp.int32, (1, LANES), 1)
    used = lane < count

    def row(k, c):
        values = jnp.concatenate(
            [pairs_ref[k, c : c + 1, :], jnp.zeros((1, LANES - count), jnp.int32)], axis=1
        )
        return values

    low = jnp.where(used, row(0, 0), -1)
    low_column = jnp.broadcast_to(low, (LANES, LANES)).T
    eye = jnp.where(used & (low_column == low), 1.0, 0.0).astype(BF16)
    hot = jnp.where(mode == low, 1.0, 0.0).astype(BF16)
    pick_ref[:, :LANES] = hot
    place_ref[:LANES, :] = dot_t(eye, hot).astype(BF16)
    for k in range(variables):
        same = jnp.where(used & (low_column == row(k, 0)), 1.0, 0.0).astype(BF16)
        raised = jnp.where(mode == jnp.where(used, row(k, 1), -1), 1.0, 0.0).astype(BF16)
        levels = jnp.broadcast_to(jnp.where(used, row(k, 2), 0).astype(F32), (16, LANES)).astype(BF16)
        at = (k + 1) * LANES
        pick_ref[:, at : at + LANES] = dot_t(raised, same).astype(BF16)
        place_ref[at : at + LANES, :] = dot_t(same, raised).astype(BF16)
        level_ref[k * 8 : (k + 1) * 8, :] = jnp.sqrt(dot_t(levels, same)[:8])


def pack_kernel(modes, f_hbm, mean_hbm, kl_hbm, low_ref, high_ref, *refs):
    sends, (first_ref, last_ref), (f_ref, mean_ref, kl_ref, sems) = refs[:3], refs[3:5], refs[5:]
    fetch((f_hbm, mean_hbm, kl_hbm), (f_ref, mean_ref, kl_ref), sems)
    pack_rows(modes, f_ref, mean_ref, kl_ref, low_ref, high_ref, sends, first_ref, last_ref)


def first_kernel(modes, passed, low_ref, high_ref, pairs_hbm, *refs):
    given, (pairs_ref, picked_ref, sems) = refs[passed : passed + 6], refs[2 * passed + 6 :]

    @pl.when(early())
    def _():
        fetch((pairs_hbm,), (pairs_ref,), sems)
        inner(modes, low_ref, high_ref, pairs_ref, *given, picked_ref)


def later_kernel(modes, low_ref, high_ref, pairs_hbm, *refs):
    given, (pairs_ref, picked_ref, sems) = refs[:6], refs[6:]

    @pl.when(jnp.logical_not(early()))
    def _():
        fetch((pairs_hbm,), (pairs_ref,), sems)
        inner(modes, low_ref, high_ref, pairs_ref, *given, picked_ref)


def inner(modes, a_ref, b_ref, pairs_ref, pick_ref, place_ref, level_ref, side_ref, low_ref, center_ref, picked_ref):
    variables = pairs_ref.shape[0]
    tables(pairs_ref, pick_ref, place_ref, level_ref)

    u = jnp.concatenate([modes_of(a_ref, modes), modes_of(b_ref, modes)], axis=0)
    c = jnp.concatenate([coefs_of(a_ref), coefs_of(b_ref)], axis=0)
    both = dot(split(u), pick_ref[...])
    picked_ref[...] = both[:CELLS] + both[CELLS:]

    face_y = 0.5 * (c[:ROW_CELLS] + c[ROW_CELLS:])
    zero = jnp.zeros((COLS, LANES), F32)

    def up_z(x):
        return jnp.concatenate(
            [x[COLS:ROW_CELLS], zero, x[ROW_CELLS + COLS :], zero], axis=0
        )

    def down_z(x):
        return jnp.concatenate(
            [zero, x[: ROW_CELLS - COLS], zero, x[ROW_CELLS : CELLS - COLS]], axis=0
        )

    face_z = 0.5 * (c + up_z(c))
    cell = lax.broadcasted_iota(jnp.int32, (CELLS, LANES), 0)
    not_last = lax.rem(cell, COLS) < COLS - 1
    face_x = jnp.where(not_last, 0.5 * (c + pltpu.roll(c, CELLS - 1, axis=0)), 0.0)

    def weighted(k, dy, dz, dx):
        fy = column(face_y, k) * dy
        fz = column(face_z, k) * dz
        fx = column(face_x, k) * dx
        net = fz - down_z(fz) + fx - pltpu.roll(fx, 1, axis=0)
        return net + jnp.concatenate([fy, -fy], axis=0)

    def diffs(x):
        return (
            x[:ROW_CELLS] - x[ROW_CELLS:],
            x - up_z(x),
            x - pltpu.roll(x, CELLS - 1, axis=0),
        )

    for t in range(WIDTH // LANES):
        lanes = slice(t * LANES, (t + 1) * LANES)
        x = u[:, lanes]
        center_ref[:, lanes] = weighted(0, *diffs(x))

    low_diffs = diffs(picked_ref[:, :LANES])
    low_sum = jnp.zeros((CELLS, LANES), F32)
    for k in range(1, variables + 1):
        out = slice((k - 1) * LANES, k * LANES)
        side_ref[:, out] = weighted(k, *low_diffs)
        level = level_ref[(k - 1) * 8 : (k - 1) * 8 + 1, :]
        low_sum = low_sum + level * weighted(k, *diffs(picked_ref[:, k * LANES : (k + 1) * LANES]))
    low_ref[...] = low_sum


def inner_shapes(turned_pairs):
    shape = jax.ShapeDtypeStruct
    variables = turned_pairs.shape[0]
    blocks = (variables + 1) * LANES
    return (
        shape((WIDTH, blocks), BF16),
        shape((blocks, WIDTH), BF16),
        shape((8 * variables, LANES), F32),
        shape((CELLS, variables * LANES), F32),
        shape((CELLS, LANES), F32),
        shape((CELLS, WIDTH), F32),
    )


def pack(field, mean, kl):
    shape = jax.ShapeDtypeStruct
    return pl.pallas_call(
        functools.partial(pack_kernel, field.shape[-1]),
        out_shape=(shape((ROW_CELLS, WIDTH), F32),) * 5 + (shape((GROUPS, WIDTH), F32),) * 2,
        in_specs=[HBM] * 3,
        out_specs=[IN_VMEM] * 7,
        scratch_shapes=[pltpu.VMEM(x.shape, x.dtype) for x in (field, mean, kl)] + [pltpu.SemaphoreType.DMA((3,))],
        compiler_params=pltpu.CompilerParams(vmem_limit_bytes=44 * 1024 * 1024),
        name="pack",
    )(field, mean, kl)


def inner_scratch(turned_pairs, made):
    return [
        pltpu.VMEM(turned_pairs.shape, turned_pairs.dtype),
        pltpu.VMEM((CELLS, made[0].shape[1]), F32),
        pltpu.SemaphoreType.DMA((1,)),
    ]


def first_work(modes, low, high, turned_pairs, sends):
    made = inner_shapes(turned_pairs)
    anywhere = pl.BlockSpec(memory_space=pl.ANY)
    out = pl.pallas_call(
        functools.partial(first_kernel, modes, len(sends)),
        out_shape=made + tuple(jax.ShapeDtypeStruct(x.shape, x.dtype) for x in sends),
        in_specs=[IN_VMEM, IN_VMEM, HBM] + [anywhere] * len(sends),
        out_specs=[IN_VMEM] * 6 + [anywhere] * len(sends),
        scratch_shapes=inner_scratch(turned_pairs, made),
        input_output_aliases={3 + i: 6 + i for i in range(len(sends))},
        compiler_params=pltpu.CompilerParams(vmem_limit_bytes=44 * 1024 * 1024),
        name="first_work",
    )(low, high, turned_pairs, *sends)
    return out[:6], out[6:]


def later(modes, low, high, turned_pairs):
    made = inner_shapes(turned_pairs)
    return pl.pallas_call(
        functools.partial(later_kernel, modes),
        out_shape=made,
        in_specs=[IN_VMEM, IN_VMEM, HBM],
        out_specs=[IN_VMEM] * 6,
        scratch_shapes=inner_scratch(turned_pairs, made),
        compiler_params=pltpu.CompilerParams(vmem_limit_bytes=44 * 1024 * 1024),
        name="later",
    )(low, high, turned_pairs)


def outer_kernel(modes, *refs):
    rows, parts, parts_then = refs[:9], refs[9:15], refs[15:21]
    out_ref, terms_ref = refs[21:]
    for mine, given in ((early(), parts), (jnp.logical_not(early()), parts_then)):

        @pl.when(mine)
        def _(given=given):
            outer_body(modes, *rows, *given, out_ref, terms_ref)


def outer_body(modes, low_ref, high_ref, rows1_ref, rows2_ref, rows3_ref, left_ref, right_ref, left_then_ref,
               right_then_ref, pick_ref, place_ref, level_ref, side_ref, low_sum_ref, center_ref,
               out_ref, terms_ref):
    variables = side_ref.shape[1] // LANES
    own = jnp.concatenate([low_ref[...], high_ref[...]], axis=0)

    def strip(x):
        at = [g * COLS for g in range(GROUPS)] + [(g + 1) * COLS - 1 for g in range(GROUPS)]
        return jnp.concatenate([x[i : i + 1] for i in at], axis=0)

    def coefs(x):
        return x[:, WIDTH - LANES :]

    mine = jnp.concatenate([own, strip(own)], axis=0)
    given = (rows1_ref[...], rows2_ref[...], rows3_ref[...])
    before, behind = (pick_from(given, which) for which in comes_in())
    left = jnp.where(columns_late(), left_then_ref[...], left_ref[...])
    right = jnp.where(columns_late(), right_then_ref[...], right_ref[...])
    theirs = jnp.concatenate([before, behind, left, right], axis=0)
    lane = lax.broadcasted_iota(jnp.int32, mine.shape, 1)
    d = jnp.where(lane < modes, mine - theirs, 0.0)
    face = 0.5 * (coefs(mine) + coefs(theirs))
    row = lax.broadcasted_iota(jnp.int32, face.shape, 0)
    end = (lax.axis_index("wide") == 0) & (row < ROW_CELLS)
    end |= (lax.axis_index("narrow") == 0) & (row >= CELLS) & (row < CELLS + GROUPS)
    face = jnp.where(end, 0.0, face)
    count = face.shape[0]

    def with_own(ref, lanes, value):
        return jnp.concatenate([ref[:, lanes] + value[:CELLS], value[CELLS:]], axis=0)

    both = dot(split(d), pick_ref[...])
    picked = both[:count] + both[count:]
    low = picked[:, :LANES]
    low_sum = jnp.zeros_like(low)
    for k in range(1, variables + 1):
        level = level_ref[(k - 1) * 8 : (k - 1) * 8 + 1, :]
        f = column(face, k)
        low_sum = low_sum + level * (f * picked[:, k * LANES : (k + 1) * LANES])
        side = level * with_own(side_ref, slice((k - 1) * LANES, k * LANES), f * low)
        terms_ref[:, k * LANES : (k + 1) * LANES] = split(side)
    terms_ref[:, :LANES] = split(with_own(low_sum_ref, slice(0, LANES), low_sum))
    spread = dot(terms_ref[...], place_ref[...])
    f = column(face, 0)
    f = jnp.concatenate([f] * (WIDTH // LANES), axis=1)
    total = f * d + spread[:count] + spread[count:]
    inner_rows = center_ref[...] + total[:CELLS]
    for r in range(ROWS):
        out_ref[r] = inner_rows[r * ROW_CELLS : (r + 1) * ROW_CELLS, :modes]
    for g in range(GROUPS):
        r, z = divmod(g, DEPTH)
        for x, i in ((0, CELLS + g), (COLS - 1, CELLS + GROUPS + g)):
            out_ref[r, z * COLS + x : z * COLS + x + 1, :] += total[i : i + 1, :modes]


def outer(modes, low, high, rows, columns, parts, parts_then):
    vmem = pl.BlockSpec(memory_space=pltpu.VMEM)
    blocks = parts[0].shape[1]
    edges = (low, high, *rows, *columns)
    return pl.pallas_call(
        functools.partial(outer_kernel, modes),
        out_shape=jax.ShapeDtypeStruct((ROWS, ROW_CELLS, modes), F32),
        in_specs=[vmem] * 21,
        out_specs=vmem,
        scratch_shapes=[pltpu.VMEM((2 * (CELLS + 2 * GROUPS), blocks), BF16)],
        compiler_params=pltpu.CompilerParams(vmem_limit_bytes=40 * 1024 * 1024),
        name="outer",
    )(*edges, *parts, *parts_then)


def held(x):
    return pltpu.with_memory_space_constraint(x, pltpu.HBM)


RUN = 8
LAST = RUN - 1


def early():
    return lax.rem(lax.axis_index("wide"), RUN) < 2


def columns_late():
    at = lax.rem(lax.axis_index("wide"), RUN)
    return (at == 2) | (at == LAST)


def goes_up():
    at = lax.rem(lax.axis_index("wide"), RUN)
    return at == LAST, at != 1, at == 1


def comes_in():
    at = lax.rem(lax.axis_index("wide"), RUN)
    before = jnp.where(at == 0, 0, jnp.where(at == 2, 2, 1))
    behind = jnp.where(at >= LAST - 1, 2, jnp.where(at == 0, 1, 0))
    return before, behind


def pick_from(given, which):
    return jnp.where(which == 0, given[0], jnp.where(which == 1, given[1], given[2]))


def steps(turn, at):
    if turn == 0:
        return 1 if at == LAST else -1 if at >= 2 else 0
    if turn == 1:
        return -1 if at == 1 else 1 if at < LAST else 0
    return {0: -1, 1: 1, LAST: -1}.get(at, 0)


def send_rows(block, turn):
    size = lax.axis_size("wide")
    route = [(i, i + steps(turn, i % RUN)) for i in range(size) if steps(turn, i % RUN)]
    return lax.ppermute(block, "wide", [(i, j) for i, j in route if 0 <= j < size])


def send_columns(block, by, is_late):
    wide, narrow = lax.axis_size("wide"), lax.axis_size("narrow")
    route = [
        (w * narrow + n, w * narrow + n + by)
        for w in range(wide)
        for n in range(narrow)
        if (w % RUN in (2, LAST)) == is_late and 0 <= n + by < narrow
    ]
    return lax.ppermute(block, ("wide", "narrow"), route)


def per_device(chaos_field, mean_conductivity, kl_fields, pairs):
    modes = chaos_field.shape[-1]
    field = chaos_field.reshape(ROWS, ROW_CELLS, modes)
    turned = held(pairs.transpose(0, 2, 1))
    low, high, send1, send2, send3, first, last = pack(held(field), held(mean_conductivity), held(kl_fields))
    rows1 = send_rows(send1, 0)
    parts, (send2, send3, first, last) = first_work(modes, low, high, turned, (send2, send3, first, last))
    left = send_columns(last, 1, False)
    right = send_columns(first, -1, False)
    rows2 = send_rows(send2, 1)
    send3, left, right, rows1 = lax.optimization_barrier((send3, left, right, rows1))
    rows3 = send_rows(send3, 2)
    left_then = send_columns(last, 1, True)
    right_then = send_columns(first, -1, True)
    parts_then = later(modes, low, high, turned)
    columns = (left, right, left_then, right_then)
    out = outer(modes, low, high, (rows1, rows2, rows3), columns, parts, parts_then)
    return out.reshape(chaos_field.shape)


def solution(mesh):
    placed = (
        P("wide", None, "narrow", None),
        P("wide", None, "narrow"),
        P(None, "wide", None, "narrow"),
        P(),
    )
    return jax.shard_map(
        per_device,
        mesh=mesh,
        in_specs=placed,
        out_specs=P("wide", None, "narrow", None),
        check_vma=False,
    )
```

```python
import functools

import jax
import jax.numpy as jnp
from jax import lax
from jax.experimental import pallas as pl
from jax.experimental.pallas import tpu as pltpu
from jax.sharding import PartitionSpec as P

F32, BF16 = jnp.float32, jnp.bfloat16
LANES = 128
ROWS, DEPTH, COLS = 2, 4, 16
ROW_CELLS = DEPTH * COLS
CELLS = ROWS * ROW_CELLS
GROUPS = ROWS * DEPTH
WIDTH = 512
HBM = pl.BlockSpec(memory_space=pltpu.HBM)
IN_VMEM = pl.BlockSpec(memory_space=pltpu.VMEM)
COEF = 72


def split(x):
    hi = x.astype(BF16)
    lo = (x - hi.astype(F32)).astype(BF16)
    return jnp.concatenate([hi, lo], axis=0)


def dot(a, b):
    return jnp.dot(a, b, preferred_element_type=F32)


def dot_t(a, b):
    return lax.dot_general(a, b, (((1,), (1,)), ((), ())), preferred_element_type=F32)


def fetch(sources, targets, sems):
    copies = [pltpu.make_async_copy(s, t, sems.at[i]) for i, (s, t) in enumerate(zip(sources, targets))]
    for copy in copies:
        copy.start()
    for copy in copies:
        copy.wait()


def pack_rows(modes, f_ref, mean_ref, kl_ref, low_ref, high_ref, first_ref, last_ref):
    variables = kl_ref.shape[0]
    slabs = []
    for g in range(GROUPS):
        r, z = divmod(g, DEPTH)
        slabs.append(mean_ref[r, z : z + 1, :])
        slabs.append(kl_ref[:, r, z, :])
        slabs.append(jnp.zeros((COLS - 1 - variables, COLS), F32))
    stacked = jnp.concatenate(slabs, axis=0)
    stacked = jnp.concatenate([stacked, jnp.zeros((CELLS, LANES - COLS), F32)], axis=1)
    turned = stacked.T[:COLS]
    lane = lax.broadcasted_iota(jnp.int32, (COLS, LANES), 1)
    inside = (lane >= COEF) & (lane < COEF + variables + 1)
    behind = WIDTH - LANES
    for g in range(GROUPS):
        r, z = divmod(g, DEPTH)
        part = pltpu.roll(turned, (COEF - g * COLS) % LANES, axis=1)
        row = (low_ref, high_ref)[r]
        row[z * COLS : (z + 1) * COLS, behind:] = jnp.where(inside, part, 0.0)
    low_ref[:, :modes] = f_ref[0]
    high_ref[:, :modes] = f_ref[1]
    for g in range(GROUPS):
        r, z = divmod(g, DEPTH)
        row, at = (low_ref, high_ref)[r], z * COLS
        first_ref[g : g + 1, :] = row[at : at + 1, :]
        last_ref[g : g + 1, :] = row[at + COLS - 1 : at + COLS, :]


def modes_of(ref, modes):
    x = ref[...]
    lane = lax.broadcasted_iota(jnp.int32, x.shape, 1)
    return jnp.where(lane < modes, x, 0.0)


def coefs_of(ref):
    return ref[:, WIDTH - LANES :]


def column(coefs, k):
    return jnp.broadcast_to(coefs[:, COEF + k : COEF + k + 1], coefs.shape)


def tables(pairs_ref, pick_ref, place_ref, level_ref):
    variables, _, count = pairs_ref.shape
    mode = lax.broadcasted_iota(jnp.int32, (WIDTH, LANES), 0)
    lane = lax.broadcasted_iota(jnp.int32, (1, LANES), 1)
    used = lane < count

    def row(k, c):
        values = jnp.concatenate(
            [pairs_ref[k, c : c + 1, :], jnp.zeros((1, LANES - count), jnp.int32)], axis=1
        )
        return values

    low = jnp.where(used, row(0, 0), -1)
    low_column = jnp.broadcast_to(low, (LANES, LANES)).T
    eye = jnp.where(used & (low_column == low), 1.0, 0.0).astype(BF16)
    hot = jnp.where(mode == low, 1.0, 0.0).astype(BF16)
    pick_ref[:, :LANES] = hot
    place_ref[:LANES, :] = dot_t(eye, hot).astype(BF16)
    for k in range(variables):
        same = jnp.where(used & (low_column == row(k, 0)), 1.0, 0.0).astype(BF16)
        raised = jnp.where(mode == jnp.where(used, row(k, 1), -1), 1.0, 0.0).astype(BF16)
        levels = jnp.broadcast_to(jnp.where(used, row(k, 2), 0).astype(F32), (16, LANES)).astype(BF16)
        at = (k + 1) * LANES
        pick_ref[:, at : at + LANES] = dot_t(raised, same).astype(BF16)
        place_ref[at : at + LANES, :] = dot_t(same, raised).astype(BF16)
        level_ref[k * 8 : (k + 1) * 8, :] = jnp.sqrt(dot_t(levels, same)[:8])


def start_kernel(modes, f_hbm, mean_hbm, kl_hbm, pairs_hbm, low_ref, high_ref, again_ref, first_ref, last_ref, *refs):
    given, (f_ref, mean_ref, kl_ref, pairs_ref, picked_ref, sems) = refs[:6], refs[6:]
    fetch((f_hbm, mean_hbm, kl_hbm), (f_ref, mean_ref, kl_ref), sems)
    pack_rows(modes, f_ref, mean_ref, kl_ref, low_ref, high_ref, first_ref, last_ref)

    again_ref[...] = high_ref[...]

    @pl.when(early())
    def _():
        fetch((pairs_hbm,), (pairs_ref,), sems)
        inner(modes, low_ref, high_ref, pairs_ref, *given, picked_ref)


def later_kernel(modes, low_ref, high_ref, pairs_hbm, *refs):
    given, (pairs_ref, picked_ref, sems) = refs[:6], refs[6:]

    @pl.when(jnp.logical_not(early()))
    def _():
        fetch((pairs_hbm,), (pairs_ref,), sems)
        inner(modes, low_ref, high_ref, pairs_ref, *given, picked_ref)


def inner(modes, a_ref, b_ref, pairs_ref, pick_ref, place_ref, level_ref, side_ref, low_ref, center_ref, picked_ref):
    variables = pairs_ref.shape[0]
    tables(pairs_ref, pick_ref, place_ref, level_ref)

    u = jnp.concatenate([modes_of(a_ref, modes), modes_of(b_ref, modes)], axis=0)
    c = jnp.concatenate([coefs_of(a_ref), coefs_of(b_ref)], axis=0)
    both = dot(split(u), pick_ref[...])
    picked_ref[...] = both[:CELLS] + both[CELLS:]

    face_y = 0.5 * (c[:ROW_CELLS] + c[ROW_CELLS:])
    zero = jnp.zeros((COLS, LANES), F32)

    def up_z(x):
        return jnp.concatenate(
            [x[COLS:ROW_CELLS], zero, x[ROW_CELLS + COLS :], zero], axis=0
        )

    def down_z(x):
        return jnp.concatenate(
            [zero, x[: ROW_CELLS - COLS], zero, x[ROW_CELLS : CELLS - COLS]], axis=0
        )

    face_z = 0.5 * (c + up_z(c))
    cell = lax.broadcasted_iota(jnp.int32, (CELLS, LANES), 0)
    not_last = lax.rem(cell, COLS) < COLS - 1
    face_x = jnp.where(not_last, 0.5 * (c + pltpu.roll(c, CELLS - 1, axis=0)), 0.0)

    def weighted(k, dy, dz, dx):
        fy = column(face_y, k) * dy
        fz = column(face_z, k) * dz
        fx = column(face_x, k) * dx
        net = fz - down_z(fz) + fx - pltpu.roll(fx, 1, axis=0)
        return net + jnp.concatenate([fy, -fy], axis=0)

    def diffs(x):
        return (
            x[:ROW_CELLS] - x[ROW_CELLS:],
            x - up_z(x),
            x - pltpu.roll(x, CELLS - 1, axis=0),
        )

    for t in range(WIDTH // LANES):
        lanes = slice(t * LANES, (t + 1) * LANES)
        x = u[:, lanes]
        center_ref[:, lanes] = weighted(0, *diffs(x))

    low_diffs = diffs(picked_ref[:, :LANES])
    low_sum = jnp.zeros((CELLS, LANES), F32)
    for k in range(1, variables + 1):
        out = slice((k - 1) * LANES, k * LANES)
        side_ref[:, out] = weighted(k, *low_diffs)
        level = level_ref[(k - 1) * 8 : (k - 1) * 8 + 1, :]
        low_sum = low_sum + level * weighted(k, *diffs(picked_ref[:, k * LANES : (k + 1) * LANES]))
    low_ref[...] = low_sum


def inner_shapes(turned_pairs):
    shape = jax.ShapeDtypeStruct
    variables = turned_pairs.shape[0]
    blocks = (variables + 1) * LANES
    return (
        shape((WIDTH, blocks), BF16),
        shape((blocks, WIDTH), BF16),
        shape((8 * variables, LANES), F32),
        shape((CELLS, variables * LANES), F32),
        shape((CELLS, LANES), F32),
        shape((CELLS, WIDTH), F32),
    )


def start(field, mean, kl, turned_pairs):
    shape = jax.ShapeDtypeStruct
    made = inner_shapes(turned_pairs)
    return pl.pallas_call(
        functools.partial(start_kernel, field.shape[-1]),
        out_shape=(
            shape((ROW_CELLS, WIDTH), F32),
            shape((ROW_CELLS, WIDTH), F32),
            shape((ROW_CELLS, WIDTH), F32),
            shape((GROUPS, WIDTH), F32),
            shape((GROUPS, WIDTH), F32),
        )
        + made,
        in_specs=[HBM] * 4,
        out_specs=[IN_VMEM] * 11,
        scratch_shapes=[pltpu.VMEM(x.shape, x.dtype) for x in (field, mean, kl, turned_pairs)]
        + [pltpu.VMEM((CELLS, made[0].shape[1]), F32), pltpu.SemaphoreType.DMA((3,))],
        compiler_params=pltpu.CompilerParams(vmem_limit_bytes=44 * 1024 * 1024),
        name="start",
    )(field, mean, kl, turned_pairs)


def later(modes, low, high, turned_pairs):
    made = inner_shapes(turned_pairs)
    return pl.pallas_call(
        functools.partial(later_kernel, modes),
        out_shape=made,
        in_specs=[IN_VMEM, IN_VMEM, HBM],
        out_specs=[IN_VMEM] * 6,
        scratch_shapes=[
            pltpu.VMEM(turned_pairs.shape, turned_pairs.dtype),
            pltpu.VMEM((CELLS, made[0].shape[1]), F32),
            pltpu.SemaphoreType.DMA((1,)),
        ],
        compiler_params=pltpu.CompilerParams(vmem_limit_bytes=44 * 1024 * 1024),
        name="later",
    )(low, high, turned_pairs)


def outer_kernel(modes, *refs):
    rows, parts, parts_then = refs[:7], refs[7:13], refs[13:19]
    out_ref, terms_ref = refs[19:]
    for mine, given in ((early(), parts), (jnp.logical_not(early()), parts_then)):

        @pl.when(mine)
        def _(given=given):
            outer_body(modes, *rows, *given, out_ref, terms_ref)


def outer_body(modes, low_ref, high_ref, run_ref, before_ref, behind_ref, left_ref, right_ref, pick_ref, place_ref,
               level_ref, side_ref, low_sum_ref, center_ref, out_ref, terms_ref):
    variables = side_ref.shape[1] // LANES
    own = jnp.concatenate([low_ref[...], high_ref[...]], axis=0)

    def strip(x):
        at = [g * COLS for g in range(GROUPS)] + [(g + 1) * COLS - 1 for g in range(GROUPS)]
        return jnp.concatenate([x[i : i + 1] for i in at], axis=0)

    def coefs(x):
        return x[:, WIDTH - LANES :]

    mine = jnp.concatenate([own, strip(own)], axis=0)
    before = jnp.where(lax.rem(lax.axis_index("wide"), RUN) == 0, run_ref[...], before_ref[...])
    theirs = jnp.concatenate([before, behind_ref[...], left_ref[...], right_ref[...]], axis=0)
    lane = lax.broadcasted_iota(jnp.int32, mine.shape, 1)
    d = jnp.where(lane < modes, mine - theirs, 0.0)
    face = 0.5 * (coefs(mine) + coefs(theirs))
    row = lax.broadcasted_iota(jnp.int32, face.shape, 0)
    end = (lax.axis_index("wide") == 0) & (row < ROW_CELLS)
    end |= (lax.axis_index("narrow") == 0) & (row >= CELLS) & (row < CELLS + GROUPS)
    face = jnp.where(end, 0.0, face)
    count = face.shape[0]

    def with_own(ref, lanes, value):
        return jnp.concatenate([ref[:, lanes] + value[:CELLS], value[CELLS:]], axis=0)

    both = dot(split(d), pick_ref[...])
    picked = both[:count] + both[count:]
    low = picked[:, :LANES]
    low_sum = jnp.zeros_like(low)
    for k in range(1, variables + 1):
        level = level_ref[(k - 1) * 8 : (k - 1) * 8 + 1, :]
        f = column(face, k)
        low_sum = low_sum + level * (f * picked[:, k * LANES : (k + 1) * LANES])
        side = level * with_own(side_ref, slice((k - 1) * LANES, k * LANES), f * low)
        terms_ref[:, k * LANES : (k + 1) * LANES] = split(side)
    terms_ref[:, :LANES] = split(with_own(low_sum_ref, slice(0, LANES), low_sum))
    spread = dot(terms_ref[...], place_ref[...])
    f = column(face, 0)
    f = jnp.concatenate([f] * (WIDTH // LANES), axis=1)
    total = f * d + spread[:count] + spread[count:]
    inner_rows = center_ref[...] + total[:CELLS]
    for r in range(ROWS):
        out_ref[r] = inner_rows[r * ROW_CELLS : (r + 1) * ROW_CELLS, :modes]
    for g in range(GROUPS):
        r, z = divmod(g, DEPTH)
        for x, i in ((0, CELLS + g), (COLS - 1, CELLS + GROUPS + g)):
            out_ref[r, z * COLS + x : z * COLS + x + 1, :] += total[i : i + 1, :modes]


def outer(modes, low, high, before_run, before, behind, left, right, parts, parts_then):
    vmem = pl.BlockSpec(memory_space=pltpu.VMEM)
    blocks = parts[0].shape[1]
    edges = (low, high, before_run, before, behind, left, right)
    return pl.pallas_call(
        functools.partial(outer_kernel, modes),
        out_shape=jax.ShapeDtypeStruct((ROWS, ROW_CELLS, modes), F32),
        in_specs=[vmem] * 19,
        out_specs=vmem,
        scratch_shapes=[pltpu.VMEM((2 * (CELLS + 2 * GROUPS), blocks), BF16)],
        compiler_params=pltpu.CompilerParams(vmem_limit_bytes=40 * 1024 * 1024),
        name="outer",
    )(*edges, *parts, *parts_then)


def held(x):
    return pltpu.with_memory_space_constraint(x, pltpu.HBM)


def shift(block, axis, by, ends=None):
    size = lax.axis_size(axis)
    route = [(i, i + by) for i in range(size) if 0 <= i + by < size]
    if ends is not None:
        route = [(i, j) for i, j in route if (i % RUN == RUN - 1) == ends]
    return lax.ppermute(block, axis, route)


RUN = 8


def early():
    return lax.rem(lax.axis_index("wide"), RUN) < 2


def per_device(chaos_field, mean_conductivity, kl_fields, pairs):
    modes = chaos_field.shape[-1]
    field = chaos_field.reshape(ROWS, ROW_CELLS, modes)
    turned = held(pairs.transpose(0, 2, 1))
    low, high, again, first, last, *parts = start(held(field), held(mean_conductivity), held(kl_fields), turned)
    before_run = shift(again, "wide", 1, ends=True)
    before = shift(high, "wide", 1, ends=False)
    behind = shift(low, "wide", -1)
    left = shift(last, "narrow", 1)
    right = shift(first, "narrow", -1)
    parts_then = later(modes, low, high, turned)
    out = outer(modes, low, high, before_run, before, behind, left, right, parts, parts_then)
    return out.reshape(chaos_field.shape)


def solution(mesh):
    placed = (
        P("wide", None, "narrow", None),
        P("wide", None, "narrow"),
        P(None, "wide", None, "narrow"),
        P(),
    )
    return jax.shard_map(
        per_device,
        mesh=mesh,
        in_specs=placed,
        out_specs=P("wide", None, "narrow", None),
        check_vma=False,
    )
```

```python
import functools

import jax
import jax.numpy as jnp
from jax import lax
from jax.experimental import pallas as pl
from jax.experimental.pallas import tpu as pltpu
from jax.sharding import PartitionSpec as P

F32, BF16 = jnp.float32, jnp.bfloat16
LANES = 128
ROWS, DEPTH, COLS = 2, 4, 16
ROW_CELLS = DEPTH * COLS
CELLS = ROWS * ROW_CELLS
GROUPS = ROWS * DEPTH
WIDTH = 512
HBM = pl.BlockSpec(memory_space=pltpu.HBM)
IN_VMEM = pl.BlockSpec(memory_space=pltpu.VMEM)
COEF = 72


def split(x):
    hi = x.astype(BF16)
    lo = (x - hi.astype(F32)).astype(BF16)
    return jnp.concatenate([hi, lo], axis=0)


def dot(a, b):
    return jnp.dot(a, b, preferred_element_type=F32)


def dot_t(a, b):
    return lax.dot_general(a, b, (((1,), (1,)), ((), ())), preferred_element_type=F32)


def fetch(sources, targets, sems):
    copies = [pltpu.make_async_copy(s, t, sems.at[i]) for i, (s, t) in enumerate(zip(sources, targets))]
    for copy in copies:
        copy.start()
    for copy in copies:
        copy.wait()


def pack_rows(modes, f_ref, mean_ref, kl_ref, low_ref, high_ref, first_ref, last_ref):
    variables = kl_ref.shape[0]
    slabs = []
    for g in range(GROUPS):
        r, z = divmod(g, DEPTH)
        slabs.append(mean_ref[r, z : z + 1, :])
        slabs.append(kl_ref[:, r, z, :])
        slabs.append(jnp.zeros((COLS - 1 - variables, COLS), F32))
    stacked = jnp.concatenate(slabs, axis=0)
    stacked = jnp.concatenate([stacked, jnp.zeros((CELLS, LANES - COLS), F32)], axis=1)
    turned = stacked.T[:COLS]
    lane = lax.broadcasted_iota(jnp.int32, (COLS, LANES), 1)
    inside = (lane >= COEF) & (lane < COEF + variables + 1)
    behind = WIDTH - LANES
    for g in range(GROUPS):
        r, z = divmod(g, DEPTH)
        part = pltpu.roll(turned, (COEF - g * COLS) % LANES, axis=1)
        row = (low_ref, high_ref)[r]
        row[z * COLS : (z + 1) * COLS, behind:] = jnp.where(inside, part, 0.0)
    low_ref[:, :modes] = f_ref[0]
    high_ref[:, :modes] = f_ref[1]
    for g in range(GROUPS):
        r, z = divmod(g, DEPTH)
        row, at = (low_ref, high_ref)[r], z * COLS
        first_ref[g : g + 1, :] = row[at : at + 1, :]
        last_ref[g : g + 1, :] = row[at + COLS - 1 : at + COLS, :]


def modes_of(ref, modes):
    x = ref[...]
    lane = lax.broadcasted_iota(jnp.int32, x.shape, 1)
    return jnp.where(lane < modes, x, 0.0)


def coefs_of(ref):
    return ref[:, WIDTH - LANES :]


def column(coefs, k):
    return jnp.broadcast_to(coefs[:, COEF + k : COEF + k + 1], coefs.shape)


def tables(pairs_ref, pick_ref, place_ref, level_ref):
    variables, _, count = pairs_ref.shape
    mode = lax.broadcasted_iota(jnp.int32, (WIDTH, LANES), 0)
    lane = lax.broadcasted_iota(jnp.int32, (1, LANES), 1)
    used = lane < count

    def row(k, c):
        values = jnp.concatenate(
            [pairs_ref[k, c : c + 1, :], jnp.zeros((1, LANES - count), jnp.int32)], axis=1
        )
        return values

    low = jnp.where(used, row(0, 0), -1)
    low_column = jnp.broadcast_to(low, (LANES, LANES)).T
    eye = jnp.where(used & (low_column == low), 1.0, 0.0).astype(BF16)
    hot = jnp.where(mode == low, 1.0, 0.0).astype(BF16)
    pick_ref[:, :LANES] = hot
    place_ref[:LANES, :] = dot_t(eye, hot).astype(BF16)
    for k in range(variables):
        same = jnp.where(used & (low_column == row(k, 0)), 1.0, 0.0).astype(BF16)
        raised = jnp.where(mode == jnp.where(used, row(k, 1), -1), 1.0, 0.0).astype(BF16)
        levels = jnp.broadcast_to(jnp.where(used, row(k, 2), 0).astype(F32), (16, LANES)).astype(BF16)
        at = (k + 1) * LANES
        pick_ref[:, at : at + LANES] = dot_t(raised, same).astype(BF16)
        place_ref[at : at + LANES, :] = dot_t(same, raised).astype(BF16)
        level_ref[k * 8 : (k + 1) * 8, :] = jnp.sqrt(dot_t(levels, same)[:8])


def start_kernel(modes, f_hbm, mean_hbm, kl_hbm, pairs_hbm, low_ref, high_ref, rows1_ref, rows2_ref, columns1_ref, columns2_ref, *refs):
    given, (f_ref, mean_ref, kl_ref, pairs_ref, picked_ref, first_ref, last_ref, sems) = refs[:6], refs[6:]
    fetch((f_hbm, mean_hbm, kl_hbm), (f_ref, mean_ref, kl_ref), sems)
    pack_rows(modes, f_ref, mean_ref, kl_ref, low_ref, high_ref, first_ref, last_ref)
    low, high, first, last = low_ref[...], high_ref[...], first_ref[...], last_ref[...]
    rows1_ref[...] = jnp.where(odd("wide"), high, low)
    rows2_ref[...] = jnp.where(odd("wide"), low, high)
    columns1_ref[...] = jnp.where(odd("narrow"), last, first)
    columns2_ref[...] = jnp.where(odd("narrow"), first, last)

    @pl.when(early())
    def _():
        fetch((pairs_hbm,), (pairs_ref,), sems)
        inner(modes, low_ref, high_ref, pairs_ref, *given, picked_ref)


def later_kernel(modes, low_ref, high_ref, pairs_hbm, *refs):
    given, (pairs_ref, picked_ref, sems) = refs[:6], refs[6:]

    @pl.when(jnp.logical_not(early()))
    def _():
        fetch((pairs_hbm,), (pairs_ref,), sems)
        inner(modes, low_ref, high_ref, pairs_ref, *given, picked_ref)


def inner(modes, a_ref, b_ref, pairs_ref, pick_ref, place_ref, level_ref, side_ref, low_ref, center_ref, picked_ref):
    variables = pairs_ref.shape[0]
    tables(pairs_ref, pick_ref, place_ref, level_ref)

    u = jnp.concatenate([modes_of(a_ref, modes), modes_of(b_ref, modes)], axis=0)
    c = jnp.concatenate([coefs_of(a_ref), coefs_of(b_ref)], axis=0)
    both = dot(split(u), pick_ref[...])
    picked_ref[...] = both[:CELLS] + both[CELLS:]

    face_y = 0.5 * (c[:ROW_CELLS] + c[ROW_CELLS:])
    zero = jnp.zeros((COLS, LANES), F32)

    def up_z(x):
        return jnp.concatenate(
            [x[COLS:ROW_CELLS], zero, x[ROW_CELLS + COLS :], zero], axis=0
        )

    def down_z(x):
        return jnp.concatenate(
            [zero, x[: ROW_CELLS - COLS], zero, x[ROW_CELLS : CELLS - COLS]], axis=0
        )

    face_z = 0.5 * (c + up_z(c))
    cell = lax.broadcasted_iota(jnp.int32, (CELLS, LANES), 0)
    not_last = lax.rem(cell, COLS) < COLS - 1
    face_x = jnp.where(not_last, 0.5 * (c + pltpu.roll(c, CELLS - 1, axis=0)), 0.0)

    def weighted(k, dy, dz, dx):
        fy = column(face_y, k) * dy
        fz = column(face_z, k) * dz
        fx = column(face_x, k) * dx
        net = fz - down_z(fz) + fx - pltpu.roll(fx, 1, axis=0)
        return net + jnp.concatenate([fy, -fy], axis=0)

    def diffs(x):
        return (
            x[:ROW_CELLS] - x[ROW_CELLS:],
            x - up_z(x),
            x - pltpu.roll(x, CELLS - 1, axis=0),
        )

    for t in range(WIDTH // LANES):
        lanes = slice(t * LANES, (t + 1) * LANES)
        x = u[:, lanes]
        center_ref[:, lanes] = weighted(0, *diffs(x))

    low_diffs = diffs(picked_ref[:, :LANES])
    low_sum = jnp.zeros((CELLS, LANES), F32)
    for k in range(1, variables + 1):
        out = slice((k - 1) * LANES, k * LANES)
        side_ref[:, out] = weighted(k, *low_diffs)
        level = level_ref[(k - 1) * 8 : (k - 1) * 8 + 1, :]
        low_sum = low_sum + level * weighted(k, *diffs(picked_ref[:, k * LANES : (k + 1) * LANES]))
    low_ref[...] = low_sum


def inner_shapes(turned_pairs):
    shape = jax.ShapeDtypeStruct
    variables = turned_pairs.shape[0]
    blocks = (variables + 1) * LANES
    return (
        shape((WIDTH, blocks), BF16),
        shape((blocks, WIDTH), BF16),
        shape((8 * variables, LANES), F32),
        shape((CELLS, variables * LANES), F32),
        shape((CELLS, LANES), F32),
        shape((CELLS, WIDTH), F32),
    )


def start(field, mean, kl, turned_pairs):
    shape = jax.ShapeDtypeStruct
    made = inner_shapes(turned_pairs)
    return pl.pallas_call(
        functools.partial(start_kernel, field.shape[-1]),
        out_shape=(shape((ROW_CELLS, WIDTH), F32),) * 4 + (shape((GROUPS, WIDTH), F32),) * 2
        + made,
        in_specs=[HBM] * 4,
        out_specs=[IN_VMEM] * 12,
        scratch_shapes=[pltpu.VMEM(x.shape, x.dtype) for x in (field, mean, kl, turned_pairs)]
        + [pltpu.VMEM((CELLS, made[0].shape[1]), F32)]
        + [pltpu.VMEM((GROUPS, WIDTH), F32)] * 2
        + [pltpu.SemaphoreType.DMA((3,))],
        compiler_params=pltpu.CompilerParams(vmem_limit_bytes=44 * 1024 * 1024),
        name="start",
    )(field, mean, kl, turned_pairs)


def later(modes, low, high, turned_pairs):
    made = inner_shapes(turned_pairs)
    return pl.pallas_call(
        functools.partial(later_kernel, modes),
        out_shape=made,
        in_specs=[IN_VMEM, IN_VMEM, HBM],
        out_specs=[IN_VMEM] * 6,
        scratch_shapes=[
            pltpu.VMEM(turned_pairs.shape, turned_pairs.dtype),
            pltpu.VMEM((CELLS, made[0].shape[1]), F32),
            pltpu.SemaphoreType.DMA((1,)),
        ],
        compiler_params=pltpu.CompilerParams(vmem_limit_bytes=44 * 1024 * 1024),
        cost_estimate=pl.CostEstimate(flops=2_000_000_000, bytes_accessed=10_000_000, transcendentals=0),
        name="later",
    )(low, high, turned_pairs)


def outer_kernel(modes, *refs):
    rows, parts, parts_then = refs[:6], refs[6:12], refs[12:18]
    out_ref, terms_ref = refs[18:]
    for mine, given in ((early(), parts), (jnp.logical_not(early()), parts_then)):

        @pl.when(mine)
        def _(given=given):
            outer_body(modes, *rows, *given, out_ref, terms_ref)


def outer_body(modes, low_ref, high_ref, rows1_ref, rows2_ref, columns1_ref, columns2_ref, pick_ref, place_ref, level_ref,
               side_ref, low_sum_ref, center_ref, out_ref, terms_ref):
    variables = side_ref.shape[1] // LANES
    own = jnp.concatenate([low_ref[...], high_ref[...]], axis=0)

    def strip(x):
        at = [g * COLS for g in range(GROUPS)] + [(g + 1) * COLS - 1 for g in range(GROUPS)]
        return jnp.concatenate([x[i : i + 1] for i in at], axis=0)

    def coefs(x):
        return x[:, WIDTH - LANES :]

    mine = jnp.concatenate([own, strip(own)], axis=0)
    before = jnp.where(odd("wide"), rows2_ref[...], rows1_ref[...])
    behind = jnp.where(odd("wide"), rows1_ref[...], rows2_ref[...])
    left = jnp.where(odd("narrow"), columns2_ref[...], columns1_ref[...])
    right = jnp.where(odd("narrow"), columns1_ref[...], columns2_ref[...])
    theirs = jnp.concatenate([before, behind, left, right], axis=0)
    lane = lax.broadcasted_iota(jnp.int32, mine.shape, 1)
    d = jnp.where(lane < modes, mine - theirs, 0.0)
    face = 0.5 * (coefs(mine) + coefs(theirs))
    row = lax.broadcasted_iota(jnp.int32, face.shape, 0)
    end = (lax.axis_index("wide") == 0) & (row < ROW_CELLS)
    end |= (lax.axis_index("narrow") == 0) & (row >= CELLS) & (row < CELLS + GROUPS)
    face = jnp.where(end, 0.0, face)
    count = face.shape[0]

    def with_own(ref, lanes, value):
        return jnp.concatenate([ref[:, lanes] + value[:CELLS], value[CELLS:]], axis=0)

    both = dot(split(d), pick_ref[...])
    picked = both[:count] + both[count:]
    low = picked[:, :LANES]
    low_sum = jnp.zeros_like(low)
    for k in range(1, variables + 1):
        level = level_ref[(k - 1) * 8 : (k - 1) * 8 + 1, :]
        f = column(face, k)
        low_sum = low_sum + level * (f * picked[:, k * LANES : (k + 1) * LANES])
        side = level * with_own(side_ref, slice((k - 1) * LANES, k * LANES), f * low)
        terms_ref[:, k * LANES : (k + 1) * LANES] = split(side)
    terms_ref[:, :LANES] = split(with_own(low_sum_ref, slice(0, LANES), low_sum))
    spread = dot(terms_ref[...], place_ref[...])
    f = column(face, 0)
    f = jnp.concatenate([f] * (WIDTH // LANES), axis=1)
    total = f * d + spread[:count] + spread[count:]
    inner_rows = center_ref[...] + total[:CELLS]
    for r in range(ROWS):
        out_ref[r] = inner_rows[r * ROW_CELLS : (r + 1) * ROW_CELLS, :modes]
    for g in range(GROUPS):
        r, z = divmod(g, DEPTH)
        for x, i in ((0, CELLS + g), (COLS - 1, CELLS + GROUPS + g)):
            out_ref[r, z * COLS + x : z * COLS + x + 1, :] += total[i : i + 1, :modes]


def outer(modes, low, high, rows1, rows2, columns1, columns2, parts, parts_then):
    vmem = pl.BlockSpec(memory_space=pltpu.VMEM)
    blocks = parts[0].shape[1]
    edges = (low, high, rows1, rows2, columns1, columns2)
    return pl.pallas_call(
        functools.partial(outer_kernel, modes),
        out_shape=jax.ShapeDtypeStruct((ROWS, ROW_CELLS, modes), F32),
        in_specs=[vmem] * 18,
        out_specs=vmem,
        scratch_shapes=[pltpu.VMEM((2 * (CELLS + 2 * GROUPS), blocks), BF16)],
        compiler_params=pltpu.CompilerParams(vmem_limit_bytes=40 * 1024 * 1024),
        name="outer",
    )(*edges, *parts, *parts_then)


def held(x):
    return pltpu.with_memory_space_constraint(x, pltpu.HBM)


def odd(axis):
    return lax.rem(lax.axis_index(axis), 2) == 1


def swap(block, axis, first):
    route = []
    for i in range(first, lax.axis_size(axis) - 1, 2):
        route += [(i, i + 1), (i + 1, i)]
    return lax.ppermute(block, axis, route)


RUNS = 4


def early():
    return lax.rem(lax.div(lax.axis_index("wide"), 2), RUNS) == 0


def per_device(chaos_field, mean_conductivity, kl_fields, pairs):
    modes = chaos_field.shape[-1]
    field = chaos_field.reshape(ROWS, ROW_CELLS, modes)
    turned = held(pairs.transpose(0, 2, 1))
    low, high, rows1, rows2, columns1, columns2, *parts = start(
        held(field), held(mean_conductivity), held(kl_fields), turned
    )
    rows1 = swap(rows1, "wide", 1)
    columns1 = swap(columns1, "narrow", 1)
    columns2 = swap(columns2, "narrow", 0)
    rows2 = swap(rows2, "wide", 0)
    parts_then = later(modes, low, high, turned)
    out = outer(modes, low, high, rows1, rows2, columns1, columns2, parts, parts_then)
    return out.reshape(chaos_field.shape)


def solution(mesh):
    placed = (
        P("wide", None, "narrow", None),
        P("wide", None, "narrow"),
        P(None, "wide", None, "narrow"),
        P(),
    )
    return jax.shard_map(
        per_device,
        mesh=mesh,
        in_specs=placed,
        out_specs=P("wide", None, "narrow", None),
        check_vma=False,
    )
```

```python
import functools

import jax
import jax.numpy as jnp
from jax import lax
from jax.experimental import pallas as pl
from jax.experimental.pallas import tpu as pltpu
from jax.sharding import PartitionSpec as P

F32, BF16 = jnp.float32, jnp.bfloat16
LANES = 128
ROWS, DEPTH, COLS = 2, 4, 16
ROW_CELLS = DEPTH * COLS
CELLS = ROWS * ROW_CELLS
GROUPS = ROWS * DEPTH
WIDTH = 512
HBM = pl.BlockSpec(memory_space=pltpu.HBM)
IN_VMEM = pl.BlockSpec(memory_space=pltpu.VMEM)
COEF = 72


def split(x):
    hi = x.astype(BF16)
    lo = (x - hi.astype(F32)).astype(BF16)
    return jnp.concatenate([hi, lo], axis=0)


def dot(a, b):
    return jnp.dot(a, b, preferred_element_type=F32)


def dot_t(a, b):
    return lax.dot_general(a, b, (((1,), (1,)), ((), ())), preferred_element_type=F32)


def fetch(sources, targets, sems):
    copies = [pltpu.make_async_copy(s, t, sems.at[i]) for i, (s, t) in enumerate(zip(sources, targets))]
    for copy in copies:
        copy.start()
    for copy in copies:
        copy.wait()


def pack_rows(modes, f_ref, mean_ref, kl_ref, low_ref, high_ref, first_ref, last_ref):
    variables = kl_ref.shape[0]
    slabs = []
    for g in range(GROUPS):
        r, z = divmod(g, DEPTH)
        slabs.append(mean_ref[r, z : z + 1, :])
        slabs.append(kl_ref[:, r, z, :])
        slabs.append(jnp.zeros((COLS - 1 - variables, COLS), F32))
    stacked = jnp.concatenate(slabs, axis=0)
    stacked = jnp.concatenate([stacked, jnp.zeros((CELLS, LANES - COLS), F32)], axis=1)
    turned = stacked.T[:COLS]
    lane = lax.broadcasted_iota(jnp.int32, (COLS, LANES), 1)
    inside = (lane >= COEF) & (lane < COEF + variables + 1)
    behind = WIDTH - LANES
    for g in range(GROUPS):
        r, z = divmod(g, DEPTH)
        part = pltpu.roll(turned, (COEF - g * COLS) % LANES, axis=1)
        row = (low_ref, high_ref)[r]
        row[z * COLS : (z + 1) * COLS, behind:] = jnp.where(inside, part, 0.0)
    low_ref[:, :modes] = f_ref[0]
    high_ref[:, :modes] = f_ref[1]
    for g in range(GROUPS):
        r, z = divmod(g, DEPTH)
        row, at = (low_ref, high_ref)[r], z * COLS
        first_ref[g : g + 1, :] = row[at : at + 1, :]
        last_ref[g : g + 1, :] = row[at + COLS - 1 : at + COLS, :]


def modes_of(ref, modes):
    x = ref[...]
    lane = lax.broadcasted_iota(jnp.int32, x.shape, 1)
    return jnp.where(lane < modes, x, 0.0)


def coefs_of(ref):
    return ref[:, WIDTH - LANES :]


def column(coefs, k):
    return jnp.broadcast_to(coefs[:, COEF + k : COEF + k + 1], coefs.shape)


def tables(pairs_ref, pick_ref, place_ref, level_ref):
    variables, _, count = pairs_ref.shape
    mode = lax.broadcasted_iota(jnp.int32, (WIDTH, LANES), 0)
    lane = lax.broadcasted_iota(jnp.int32, (1, LANES), 1)
    used = lane < count

    def row(k, c):
        values = jnp.concatenate(
            [pairs_ref[k, c : c + 1, :], jnp.zeros((1, LANES - count), jnp.int32)], axis=1
        )
        return values

    low = jnp.where(used, row(0, 0), -1)
    low_column = jnp.broadcast_to(low, (LANES, LANES)).T
    eye = jnp.where(used & (low_column == low), 1.0, 0.0).astype(BF16)
    hot = jnp.where(mode == low, 1.0, 0.0).astype(BF16)
    pick_ref[:, :LANES] = hot
    place_ref[:LANES, :] = dot_t(eye, hot).astype(BF16)
    for k in range(variables):
        same = jnp.where(used & (low_column == row(k, 0)), 1.0, 0.0).astype(BF16)
        raised = jnp.where(mode == jnp.where(used, row(k, 1), -1), 1.0, 0.0).astype(BF16)
        levels = jnp.broadcast_to(jnp.where(used, row(k, 2), 0).astype(F32), (16, LANES)).astype(BF16)
        at = (k + 1) * LANES
        pick_ref[:, at : at + LANES] = dot_t(raised, same).astype(BF16)
        place_ref[at : at + LANES, :] = dot_t(same, raised).astype(BF16)
        level_ref[k * 8 : (k + 1) * 8, :] = jnp.sqrt(dot_t(levels, same)[:8])


def start_kernel(modes, f_hbm, mean_hbm, kl_hbm, pairs_hbm, low_ref, high_ref, rows1_ref, rows2_ref, columns1_ref, columns2_ref, *refs):
    given, (f_ref, mean_ref, kl_ref, pairs_ref, picked_ref, first_ref, last_ref, sems) = refs[:6], refs[6:]
    fetch((f_hbm, mean_hbm, kl_hbm), (f_ref, mean_ref, kl_ref), sems)
    pack_rows(modes, f_ref, mean_ref, kl_ref, low_ref, high_ref, first_ref, last_ref)
    low, high, first, last = low_ref[...], high_ref[...], first_ref[...], last_ref[...]
    rows1_ref[...] = jnp.where(odd("wide"), high, low)
    rows2_ref[...] = jnp.where(odd("wide"), low, high)
    columns1_ref[...] = jnp.where(odd("narrow"), last, first)
    columns2_ref[...] = jnp.where(odd("narrow"), first, last)

    @pl.when(early())
    def _():
        fetch((pairs_hbm,), (pairs_ref,), sems)
        inner(modes, low_ref, high_ref, pairs_ref, *given, picked_ref)


def later_kernel(modes, low_ref, high_ref, pairs_hbm, *refs):
    given, (pairs_ref, picked_ref, sems) = refs[:6], refs[6:]

    @pl.when(jnp.logical_not(early()))
    def _():
        fetch((pairs_hbm,), (pairs_ref,), sems)
        inner(modes, low_ref, high_ref, pairs_ref, *given, picked_ref)


def inner(modes, a_ref, b_ref, pairs_ref, pick_ref, place_ref, level_ref, side_ref, low_ref, center_ref, picked_ref):
    variables = pairs_ref.shape[0]
    tables(pairs_ref, pick_ref, place_ref, level_ref)

    u = jnp.concatenate([modes_of(a_ref, modes), modes_of(b_ref, modes)], axis=0)
    c = jnp.concatenate([coefs_of(a_ref), coefs_of(b_ref)], axis=0)
    both = dot(split(u), pick_ref[...])
    picked_ref[...] = both[:CELLS] + both[CELLS:]

    face_y = 0.5 * (c[:ROW_CELLS] + c[ROW_CELLS:])
    zero = jnp.zeros((COLS, LANES), F32)

    def up_z(x):
        return jnp.concatenate(
            [x[COLS:ROW_CELLS], zero, x[ROW_CELLS + COLS :], zero], axis=0
        )

    def down_z(x):
        return jnp.concatenate(
            [zero, x[: ROW_CELLS - COLS], zero, x[ROW_CELLS : CELLS - COLS]], axis=0
        )

    face_z = 0.5 * (c + up_z(c))
    cell = lax.broadcasted_iota(jnp.int32, (CELLS, LANES), 0)
    not_last = lax.rem(cell, COLS) < COLS - 1
    face_x = jnp.where(not_last, 0.5 * (c + pltpu.roll(c, CELLS - 1, axis=0)), 0.0)

    def weighted(k, dy, dz, dx):
        fy = column(face_y, k) * dy
        fz = column(face_z, k) * dz
        fx = column(face_x, k) * dx
        net = fz - down_z(fz) + fx - pltpu.roll(fx, 1, axis=0)
        return net + jnp.concatenate([fy, -fy], axis=0)

    def diffs(x):
        return (
            x[:ROW_CELLS] - x[ROW_CELLS:],
            x - up_z(x),
            x - pltpu.roll(x, CELLS - 1, axis=0),
        )

    for t in range(WIDTH // LANES):
        lanes = slice(t * LANES, (t + 1) * LANES)
        x = u[:, lanes]
        center_ref[:, lanes] = weighted(0, *diffs(x))

    low_diffs = diffs(picked_ref[:, :LANES])
    low_sum = jnp.zeros((CELLS, LANES), F32)
    for k in range(1, variables + 1):
        out = slice((k - 1) * LANES, k * LANES)
        side_ref[:, out] = weighted(k, *low_diffs)
        level = level_ref[(k - 1) * 8 : (k - 1) * 8 + 1, :]
        low_sum = low_sum + level * weighted(k, *diffs(picked_ref[:, k * LANES : (k + 1) * LANES]))
    low_ref[...] = low_sum


def inner_shapes(turned_pairs):
    shape = jax.ShapeDtypeStruct
    variables = turned_pairs.shape[0]
    blocks = (variables + 1) * LANES
    return (
        shape((WIDTH, blocks), BF16),
        shape((blocks, WIDTH), BF16),
        shape((8 * variables, LANES), F32),
        shape((CELLS, variables * LANES), F32),
        shape((CELLS, LANES), F32),
        shape((CELLS, WIDTH), F32),
    )


def start(field, mean, kl, turned_pairs):
    shape = jax.ShapeDtypeStruct
    made = inner_shapes(turned_pairs)
    return pl.pallas_call(
        functools.partial(start_kernel, field.shape[-1]),
        out_shape=(shape((ROW_CELLS, WIDTH), F32),) * 4 + (shape((GROUPS, WIDTH), F32),) * 2
        + made,
        in_specs=[HBM] * 4,
        out_specs=[IN_VMEM] * 12,
        scratch_shapes=[pltpu.VMEM(x.shape, x.dtype) for x in (field, mean, kl, turned_pairs)]
        + [pltpu.VMEM((CELLS, made[0].shape[1]), F32)]
        + [pltpu.VMEM((GROUPS, WIDTH), F32)] * 2
        + [pltpu.SemaphoreType.DMA((3,))],
        compiler_params=pltpu.CompilerParams(vmem_limit_bytes=44 * 1024 * 1024),
        name="start",
    )(field, mean, kl, turned_pairs)


def later(modes, low, high, turned_pairs):
    made = inner_shapes(turned_pairs)
    return pl.pallas_call(
        functools.partial(later_kernel, modes),
        out_shape=made,
        in_specs=[IN_VMEM, IN_VMEM, HBM],
        out_specs=[IN_VMEM] * 6,
        scratch_shapes=[
            pltpu.VMEM(turned_pairs.shape, turned_pairs.dtype),
            pltpu.VMEM((CELLS, made[0].shape[1]), F32),
            pltpu.SemaphoreType.DMA((1,)),
        ],
        compiler_params=pltpu.CompilerParams(vmem_limit_bytes=44 * 1024 * 1024),
        name="later",
    )(low, high, turned_pairs)


def outer_kernel(modes, *refs):
    rows, parts, parts_then = refs[:6], refs[6:12], refs[12:18]
    out_ref, terms_ref = refs[18:]
    for mine, given in ((early(), parts), (jnp.logical_not(early()), parts_then)):

        @pl.when(mine)
        def _(given=given):
            outer_body(modes, *rows, *given, out_ref, terms_ref)


def outer_body(modes, low_ref, high_ref, rows1_ref, rows2_ref, columns1_ref, columns2_ref, pick_ref, place_ref, level_ref,
               side_ref, low_sum_ref, center_ref, out_ref, terms_ref):
    variables = side_ref.shape[1] // LANES
    own = jnp.concatenate([low_ref[...], high_ref[...]], axis=0)

    def strip(x):
        at = [g * COLS for g in range(GROUPS)] + [(g + 1) * COLS - 1 for g in range(GROUPS)]
        return jnp.concatenate([x[i : i + 1] for i in at], axis=0)

    def coefs(x):
        return x[:, WIDTH - LANES :]

    mine = jnp.concatenate([own, strip(own)], axis=0)
    before = jnp.where(odd("wide"), rows2_ref[...], rows1_ref[...])
    behind = jnp.where(odd("wide"), rows1_ref[...], rows2_ref[...])
    left = jnp.where(odd("narrow"), columns2_ref[...], columns1_ref[...])
    right = jnp.where(odd("narrow"), columns1_ref[...], columns2_ref[...])
    theirs = jnp.concatenate([before, behind, left, right], axis=0)
    lane = lax.broadcasted_iota(jnp.int32, mine.shape, 1)
    d = jnp.where(lane < modes, mine - theirs, 0.0)
    face = 0.5 * (coefs(mine) + coefs(theirs))
    row = lax.broadcasted_iota(jnp.int32, face.shape, 0)
    end = (lax.axis_index("wide") == 0) & (row < ROW_CELLS)
    end |= (lax.axis_index("narrow") == 0) & (row >= CELLS) & (row < CELLS + GROUPS)
    face = jnp.where(end, 0.0, face)
    count = face.shape[0]

    def with_own(ref, lanes, value):
        return jnp.concatenate([ref[:, lanes] + value[:CELLS], value[CELLS:]], axis=0)

    both = dot(split(d), pick_ref[...])
    picked = both[:count] + both[count:]
    low = picked[:, :LANES]
    low_sum = jnp.zeros_like(low)
    for k in range(1, variables + 1):
        level = level_ref[(k - 1) * 8 : (k - 1) * 8 + 1, :]
        f = column(face, k)
        low_sum = low_sum + level * (f * picked[:, k * LANES : (k + 1) * LANES])
        side = level * with_own(side_ref, slice((k - 1) * LANES, k * LANES), f * low)
        terms_ref[:, k * LANES : (k + 1) * LANES] = split(side)
    terms_ref[:, :LANES] = split(with_own(low_sum_ref, slice(0, LANES), low_sum))
    spread = dot(terms_ref[...], place_ref[...])
    f = column(face, 0)
    f = jnp.concatenate([f] * (WIDTH // LANES), axis=1)
    total = f * d + spread[:count] + spread[count:]
    inner_rows = center_ref[...] + total[:CELLS]
    for r in range(ROWS):
        out_ref[r] = inner_rows[r * ROW_CELLS : (r + 1) * ROW_CELLS, :modes]
    for g in range(GROUPS):
        r, z = divmod(g, DEPTH)
        for x, i in ((0, CELLS + g), (COLS - 1, CELLS + GROUPS + g)):
            out_ref[r, z * COLS + x : z * COLS + x + 1, :] += total[i : i + 1, :modes]


def outer(modes, low, high, rows1, rows2, columns1, columns2, parts, parts_then):
    vmem = pl.BlockSpec(memory_space=pltpu.VMEM)
    blocks = parts[0].shape[1]
    edges = (low, high, rows1, rows2, columns1, columns2)
    return pl.pallas_call(
        functools.partial(outer_kernel, modes),
        out_shape=jax.ShapeDtypeStruct((ROWS, ROW_CELLS, modes), F32),
        in_specs=[vmem] * 18,
        out_specs=vmem,
        scratch_shapes=[pltpu.VMEM((2 * (CELLS + 2 * GROUPS), blocks), BF16)],
        compiler_params=pltpu.CompilerParams(vmem_limit_bytes=40 * 1024 * 1024),
        name="outer",
    )(*edges, *parts, *parts_then)


def held(x):
    return pltpu.with_memory_space_constraint(x, pltpu.HBM)


def odd(axis):
    return lax.rem(lax.axis_index(axis), 2) == 1


def swap(block, axis, first):
    route = []
    for i in range(first, lax.axis_size(axis) - 1, 2):
        route += [(i, i + 1), (i + 1, i)]
    return lax.ppermute(block, axis, route)


RUNS = 4


def early():
    return lax.rem(lax.div(lax.axis_index("wide"), 2), RUNS) == 0


def per_device(chaos_field, mean_conductivity, kl_fields, pairs):
    modes = chaos_field.shape[-1]
    field = chaos_field.reshape(ROWS, ROW_CELLS, modes)
    turned = held(pairs.transpose(0, 2, 1))
    low, high, rows1, rows2, columns1, columns2, *parts = start(
        held(field), held(mean_conductivity), held(kl_fields), turned
    )
    rows1 = swap(rows1, "wide", 1)
    columns1 = swap(columns1, "narrow", 1)
    columns2 = swap(columns2, "narrow", 0)
    rows2 = swap(rows2, "wide", 0)
    parts_then = later(modes, low, high, turned)
    out = outer(modes, low, high, rows1, rows2, columns1, columns2, parts, parts_then)
    return out.reshape(chaos_field.shape)


def solution(mesh):
    placed = (
        P("wide", None, "narrow", None),
        P("wide", None, "narrow"),
        P(None, "wide", None, "narrow"),
        P(),
    )
    return jax.shard_map(
        per_device,
        mesh=mesh,
        in_specs=placed,
        out_specs=P("wide", None, "narrow", None),
        check_vma=False,
    )
```

```python
import functools

import jax
import jax.numpy as jnp
from jax import lax
from jax.experimental import pallas as pl
from jax.experimental.pallas import tpu as pltpu
from jax.sharding import PartitionSpec as P

F32, BF16 = jnp.float32, jnp.bfloat16
LANES = 128
ROWS, DEPTH, COLS = 2, 4, 16
ROW_CELLS = DEPTH * COLS
CELLS = ROWS * ROW_CELLS
GROUPS = ROWS * DEPTH
WIDTH = 512
HBM = pl.BlockSpec(memory_space=pltpu.HBM)
IN_VMEM = pl.BlockSpec(memory_space=pltpu.VMEM)
COEF = 72


def split(x):
    hi = x.astype(BF16)
    lo = (x - hi.astype(F32)).astype(BF16)
    return jnp.concatenate([hi, lo], axis=0)


def dot(a, b):
    return jnp.dot(a, b, preferred_element_type=F32)


def dot_t(a, b):
    return lax.dot_general(a, b, (((1,), (1,)), ((), ())), preferred_element_type=F32)


def fetch(sources, targets, sems):
    copies = [pltpu.make_async_copy(s, t, sems.at[i]) for i, (s, t) in enumerate(zip(sources, targets))]
    for copy in copies:
        copy.start()
    for copy in copies:
        copy.wait()


def pack_rows(modes, f_ref, mean_ref, kl_ref, low_ref, high_ref, first_ref, last_ref):
    variables = kl_ref.shape[0]
    slabs = []
    for g in range(GROUPS):
        r, z = divmod(g, DEPTH)
        slabs.append(mean_ref[r, z : z + 1, :])
        slabs.append(kl_ref[:, r, z, :])
        slabs.append(jnp.zeros((COLS - 1 - variables, COLS), F32))
    stacked = jnp.concatenate(slabs, axis=0)
    stacked = jnp.concatenate([stacked, jnp.zeros((CELLS, LANES - COLS), F32)], axis=1)
    turned = stacked.T[:COLS]
    lane = lax.broadcasted_iota(jnp.int32, (COLS, LANES), 1)
    inside = (lane >= COEF) & (lane < COEF + variables + 1)
    behind = WIDTH - LANES
    for g in range(GROUPS):
        r, z = divmod(g, DEPTH)
        part = pltpu.roll(turned, (COEF - g * COLS) % LANES, axis=1)
        row = (low_ref, high_ref)[r]
        row[z * COLS : (z + 1) * COLS, behind:] = jnp.where(inside, part, 0.0)
    low_ref[:, :modes] = f_ref[0]
    high_ref[:, :modes] = f_ref[1]
    for g in range(GROUPS):
        r, z = divmod(g, DEPTH)
        row, at = (low_ref, high_ref)[r], z * COLS
        first_ref[g : g + 1, :] = row[at : at + 1, :]
        last_ref[g : g + 1, :] = row[at + COLS - 1 : at + COLS, :]


def modes_of(ref, modes):
    x = ref[...]
    lane = lax.broadcasted_iota(jnp.int32, x.shape, 1)
    return jnp.where(lane < modes, x, 0.0)


def coefs_of(ref):
    return ref[:, WIDTH - LANES :]


def column(coefs, k):
    return jnp.broadcast_to(coefs[:, COEF + k : COEF + k + 1], coefs.shape)


def tables(pairs_ref, pick_ref, place_ref, level_ref):
    variables, _, count = pairs_ref.shape
    mode = lax.broadcasted_iota(jnp.int32, (WIDTH, LANES), 0)
    lane = lax.broadcasted_iota(jnp.int32, (1, LANES), 1)
    used = lane < count

    def row(k, c):
        values = jnp.concatenate(
            [pairs_ref[k, c : c + 1, :], jnp.zeros((1, LANES - count), jnp.int32)], axis=1
        )
        return values

    low = jnp.where(used, row(0, 0), -1)
    low_column = jnp.broadcast_to(low, (LANES, LANES)).T
    eye = jnp.where(used & (low_column == low), 1.0, 0.0).astype(BF16)
    hot = jnp.where(mode == low, 1.0, 0.0).astype(BF16)
    pick_ref[:, :LANES] = hot
    place_ref[:LANES, :] = dot_t(eye, hot).astype(BF16)
    for k in range(variables):
        same = jnp.where(used & (low_column == row(k, 0)), 1.0, 0.0).astype(BF16)
        raised = jnp.where(mode == jnp.where(used, row(k, 1), -1), 1.0, 0.0).astype(BF16)
        levels = jnp.broadcast_to(jnp.where(used, row(k, 2), 0).astype(F32), (16, LANES)).astype(BF16)
        at = (k + 1) * LANES
        pick_ref[:, at : at + LANES] = dot_t(raised, same).astype(BF16)
        place_ref[at : at + LANES, :] = dot_t(same, raised).astype(BF16)
        level_ref[k * 8 : (k + 1) * 8, :] = jnp.sqrt(dot_t(levels, same)[:8])


def start_kernel(modes, f_hbm, mean_hbm, kl_hbm, pairs_hbm, low_ref, high_ref, rows1_ref, rows2_ref, columns1_ref, columns2_ref, *refs):
    given, (f_ref, mean_ref, kl_ref, pairs_ref, picked_ref, first_ref, last_ref, sems) = refs[:6], refs[6:]
    fetch((f_hbm, mean_hbm, kl_hbm), (f_ref, mean_ref, kl_ref), sems)
    pack_rows(modes, f_ref, mean_ref, kl_ref, low_ref, high_ref, first_ref, last_ref)
    low, high, first, last = low_ref[...], high_ref[...], first_ref[...], last_ref[...]
    rows1_ref[...] = jnp.where(odd("wide"), high, low)
    rows2_ref[...] = jnp.where(odd("wide"), low, high)
    columns1_ref[...] = jnp.where(odd("narrow"), first, last)
    columns2_ref[...] = jnp.where(odd("narrow"), last, first)

    @pl.when(early())
    def _():
        fetch((pairs_hbm,), (pairs_ref,), sems)
        inner(modes, low_ref, high_ref, pairs_ref, *given, picked_ref)


def later_kernel(modes, low_ref, high_ref, pairs_hbm, *refs):
    given, (pairs_ref, picked_ref, sems) = refs[:6], refs[6:]

    @pl.when(jnp.logical_not(early()))
    def _():
        fetch((pairs_hbm,), (pairs_ref,), sems)
        inner(modes, low_ref, high_ref, pairs_ref, *given, picked_ref)


def inner(modes, a_ref, b_ref, pairs_ref, pick_ref, place_ref, level_ref, side_ref, low_ref, center_ref, picked_ref):
    variables = pairs_ref.shape[0]
    tables(pairs_ref, pick_ref, place_ref, level_ref)

    u = jnp.concatenate([modes_of(a_ref, modes), modes_of(b_ref, modes)], axis=0)
    c = jnp.concatenate([coefs_of(a_ref), coefs_of(b_ref)], axis=0)
    both = dot(split(u), pick_ref[...])
    picked_ref[...] = both[:CELLS] + both[CELLS:]

    face_y = 0.5 * (c[:ROW_CELLS] + c[ROW_CELLS:])
    zero = jnp.zeros((COLS, LANES), F32)

    def up_z(x):
        return jnp.concatenate(
            [x[COLS:ROW_CELLS], zero, x[ROW_CELLS + COLS :], zero], axis=0
        )

    def down_z(x):
        return jnp.concatenate(
            [zero, x[: ROW_CELLS - COLS], zero, x[ROW_CELLS : CELLS - COLS]], axis=0
        )

    face_z = 0.5 * (c + up_z(c))
    cell = lax.broadcasted_iota(jnp.int32, (CELLS, LANES), 0)
    not_last = lax.rem(cell, COLS) < COLS - 1
    face_x = jnp.where(not_last, 0.5 * (c + pltpu.roll(c, CELLS - 1, axis=0)), 0.0)

    def weighted(k, dy, dz, dx):
        fy = column(face_y, k) * dy
        fz = column(face_z, k) * dz
        fx = column(face_x, k) * dx
        net = fz - down_z(fz) + fx - pltpu.roll(fx, 1, axis=0)
        return net + jnp.concatenate([fy, -fy], axis=0)

    def diffs(x):
        return (
            x[:ROW_CELLS] - x[ROW_CELLS:],
            x - up_z(x),
            x - pltpu.roll(x, CELLS - 1, axis=0),
        )

    for t in range(WIDTH // LANES):
        lanes = slice(t * LANES, (t + 1) * LANES)
        x = u[:, lanes]
        center_ref[:, lanes] = weighted(0, *diffs(x))

    low_diffs = diffs(picked_ref[:, :LANES])
    low_sum = jnp.zeros((CELLS, LANES), F32)
    for k in range(1, variables + 1):
        out = slice((k - 1) * LANES, k * LANES)
        side_ref[:, out] = weighted(k, *low_diffs)
        level = level_ref[(k - 1) * 8 : (k - 1) * 8 + 1, :]
        low_sum = low_sum + level * weighted(k, *diffs(picked_ref[:, k * LANES : (k + 1) * LANES]))
    low_ref[...] = low_sum


def inner_shapes(turned_pairs):
    shape = jax.ShapeDtypeStruct
    variables = turned_pairs.shape[0]
    blocks = (variables + 1) * LANES
    return (
        shape((WIDTH, blocks), BF16),
        shape((blocks, WIDTH), BF16),
        shape((8 * variables, LANES), F32),
        shape((CELLS, variables * LANES), F32),
        shape((CELLS, LANES), F32),
        shape((CELLS, WIDTH), F32),
    )


def start(field, mean, kl, turned_pairs):
    shape = jax.ShapeDtypeStruct
    made = inner_shapes(turned_pairs)
    return pl.pallas_call(
        functools.partial(start_kernel, field.shape[-1]),
        out_shape=(shape((ROW_CELLS, WIDTH), F32),) * 4 + (shape((GROUPS, WIDTH), F32),) * 2
        + made,
        in_specs=[HBM] * 4,
        out_specs=[IN_VMEM] * 12,
        scratch_shapes=[pltpu.VMEM(x.shape, x.dtype) for x in (field, mean, kl, turned_pairs)]
        + [pltpu.VMEM((CELLS, made[0].shape[1]), F32)]
        + [pltpu.VMEM((GROUPS, WIDTH), F32)] * 2
        + [pltpu.SemaphoreType.DMA((3,))],
        compiler_params=pltpu.CompilerParams(vmem_limit_bytes=44 * 1024 * 1024),
        name="start",
    )(field, mean, kl, turned_pairs)


def later(modes, low, high, turned_pairs):
    made = inner_shapes(turned_pairs)
    return pl.pallas_call(
        functools.partial(later_kernel, modes),
        out_shape=made,
        in_specs=[IN_VMEM, IN_VMEM, HBM],
        out_specs=[IN_VMEM] * 6,
        scratch_shapes=[
            pltpu.VMEM(turned_pairs.shape, turned_pairs.dtype),
            pltpu.VMEM((CELLS, made[0].shape[1]), F32),
            pltpu.SemaphoreType.DMA((1,)),
        ],
        compiler_params=pltpu.CompilerParams(vmem_limit_bytes=44 * 1024 * 1024),
        name="later",
    )(low, high, turned_pairs)


def outer_kernel(modes, *refs):
    rows, parts, parts_then = refs[:6], refs[6:12], refs[12:18]
    out_ref, terms_ref = refs[18:]
    for mine, given in ((early(), parts), (jnp.logical_not(early()), parts_then)):

        @pl.when(mine)
        def _(given=given):
            outer_body(modes, *rows, *given, out_ref, terms_ref)


def outer_body(modes, low_ref, high_ref, rows1_ref, rows2_ref, columns1_ref, columns2_ref, pick_ref, place_ref, level_ref,
               side_ref, low_sum_ref, center_ref, out_ref, terms_ref):
    variables = side_ref.shape[1] // LANES
    own = jnp.concatenate([low_ref[...], high_ref[...]], axis=0)

    def strip(x):
        at = [g * COLS for g in range(GROUPS)] + [(g + 1) * COLS - 1 for g in range(GROUPS)]
        return jnp.concatenate([x[i : i + 1] for i in at], axis=0)

    def coefs(x):
        return x[:, WIDTH - LANES :]

    mine = jnp.concatenate([own, strip(own)], axis=0)
    before = jnp.where(odd("wide"), rows2_ref[...], rows1_ref[...])
    behind = jnp.where(odd("wide"), rows1_ref[...], rows2_ref[...])
    left = jnp.where(odd("narrow"), columns1_ref[...], columns2_ref[...])
    right = jnp.where(odd("narrow"), columns2_ref[...], columns1_ref[...])
    theirs = jnp.concatenate([before, behind, left, right], axis=0)
    lane = lax.broadcasted_iota(jnp.int32, mine.shape, 1)
    d = jnp.where(lane < modes, mine - theirs, 0.0)
    face = 0.5 * (coefs(mine) + coefs(theirs))
    row = lax.broadcasted_iota(jnp.int32, face.shape, 0)
    end = (lax.axis_index("wide") == 0) & (row < ROW_CELLS)
    end |= (lax.axis_index("narrow") == 0) & (row >= CELLS) & (row < CELLS + GROUPS)
    face = jnp.where(end, 0.0, face)
    count = face.shape[0]

    def with_own(ref, lanes, value):
        return jnp.concatenate([ref[:, lanes] + value[:CELLS], value[CELLS:]], axis=0)

    both = dot(split(d), pick_ref[...])
    picked = both[:count] + both[count:]
    low = picked[:, :LANES]
    low_sum = jnp.zeros_like(low)
    for k in range(1, variables + 1):
        level = level_ref[(k - 1) * 8 : (k - 1) * 8 + 1, :]
        f = column(face, k)
        low_sum = low_sum + level * (f * picked[:, k * LANES : (k + 1) * LANES])
        side = level * with_own(side_ref, slice((k - 1) * LANES, k * LANES), f * low)
        terms_ref[:, k * LANES : (k + 1) * LANES] = split(side)
    terms_ref[:, :LANES] = split(with_own(low_sum_ref, slice(0, LANES), low_sum))
    spread = dot(terms_ref[...], place_ref[...])
    f = column(face, 0)
    f = jnp.concatenate([f] * (WIDTH // LANES), axis=1)
    total = f * d + spread[:count] + spread[count:]
    inner_rows = center_ref[...] + total[:CELLS]
    for r in range(ROWS):
        out_ref[r] = inner_rows[r * ROW_CELLS : (r + 1) * ROW_CELLS, :modes]
    for g in range(GROUPS):
        r, z = divmod(g, DEPTH)
        for x, i in ((0, CELLS + g), (COLS - 1, CELLS + GROUPS + g)):
            out_ref[r, z * COLS + x : z * COLS + x + 1, :] += total[i : i + 1, :modes]


def outer(modes, low, high, rows1, rows2, columns1, columns2, parts, parts_then):
    vmem = pl.BlockSpec(memory_space=pltpu.VMEM)
    blocks = parts[0].shape[1]
    edges = (low, high, rows1, rows2, columns1, columns2)
    return pl.pallas_call(
        functools.partial(outer_kernel, modes),
        out_shape=jax.ShapeDtypeStruct((ROWS, ROW_CELLS, modes), F32),
        in_specs=[vmem] * 18,
        out_specs=vmem,
        scratch_shapes=[pltpu.VMEM((2 * (CELLS + 2 * GROUPS), blocks), BF16)],
        compiler_params=pltpu.CompilerParams(vmem_limit_bytes=40 * 1024 * 1024),
        name="outer",
    )(*edges, *parts, *parts_then)


def held(x):
    return pltpu.with_memory_space_constraint(x, pltpu.HBM)


def odd(axis):
    return lax.rem(lax.axis_index(axis), 2) == 1


def swap(block, axis, first):
    route = []
    for i in range(first, lax.axis_size(axis) - 1, 2):
        route += [(i, i + 1), (i + 1, i)]
    return lax.ppermute(block, axis, route)


RUNS = 4


def early():
    return lax.rem(lax.div(lax.axis_index("wide"), 2), RUNS) == 0


def per_device(chaos_field, mean_conductivity, kl_fields, pairs):
    modes = chaos_field.shape[-1]
    field = chaos_field.reshape(ROWS, ROW_CELLS, modes)
    turned = held(pairs.transpose(0, 2, 1))
    low, high, rows1, rows2, columns1, columns2, *parts = start(
        held(field), held(mean_conductivity), held(kl_fields), turned
    )
    rows1 = swap(rows1, "wide", 1)
    columns1 = swap(columns1, "narrow", 0)
    columns2 = swap(columns2, "narrow", 1)
    rows2 = swap(rows2, "wide", 0)
    parts_then = later(modes, low, high, turned)
    out = outer(modes, low, high, rows1, rows2, columns1, columns2, parts, parts_then)
    return out.reshape(chaos_field.shape)


def solution(mesh):
    placed = (
        P("wide", None, "narrow", None),
        P("wide", None, "narrow"),
        P(None, "wide", None, "narrow"),
        P(),
    )
    return jax.shard_map(
        per_device,
        mesh=mesh,
        in_specs=placed,
        out_specs=P("wide", None, "narrow", None),
        check_vma=False,
    )
```
